128 devices in a mesh: rep: 16 (over y_hi, x, core), shard: 8 (over z, y_lo).
Axes of the slice: x: 4, y: 4 (y_hi: 2, y_lo: 2; y = y_hi * 2 + y_lo), z: 4, core: 2. Of those that a mesh axis runs over, the one named last changes fastest.
Arguments:
- tokens: bfloat16 [16, 1024, 1024], P('rep', 'shard'), may hold values from -6 to 6
- input_weight: bfloat16 [1024, 3072], P('shard'), may hold values from -0.1875 to 0.1875
- query_value_bias: bfloat16 [2048], P('shard'), may hold values from -3 to 3
- output_weight: bfloat16 [1024, 1024], P('shard'), may hold values from -4 to 4
- output_bias: bfloat16 [1024], P('shard'), may hold values from -3 to 3
- expand_weight: bfloat16 [1024, 4096], P('shard'), may hold values from -0.1875 to 0.1875
- expand_bias: bfloat16 [4096], P('shard'), may hold values from -3 to 3
- reduce_weight: bfloat16 [4096, 1024], P('shard'), may hold values from -0.09375 to 0.09375
- reduce_bias: bfloat16 [1024], P('shard'), may hold values from -3 to 3
- first_gain: bfloat16 [1024], P('shard'), may hold values from 0.5 to 1.5
- first_shift: bfloat16 [1024], P('shard'), may hold values from -3 to 3
- second_gain: bfloat16 [1024], P('shard'), may hold values from 0.5 to 1.5
- second_shift: bfloat16 [1024], P('shard'), may hold values from -3 to 3
- attention_scale: bfloat16 [1024], P('shard'), may hold values from 0.5 to 2
- feedforward_scale: bfloat16 [1024], P('shard'), may hold values from 0.5 to 2
- cotangent: bfloat16 [16, 1024, 1024], P('rep', 'shard'), may hold values from -6 to 6
Outputs:
- layer_output: bfloat16 [16, 1024, 1024], P('rep', 'shard')
- tokens_adjoint: bfloat16 [16, 1024, 1024], P('rep', 'shard')
- input_weight_adjoint: float32 [1024, 3072], P('shard')
- query_value_bias_adjoint: float32 [2048], P('shard')
- output_weight_adjoint: float32 [1024, 1024], P('shard')
- output_bias_adjoint: float32 [1024], P('shard')
- expand_weight_adjoint: float32 [1024, 4096], P('shard')
- expand_bias_adjoint: float32 [4096], P('shard')
- reduce_weight_adjoint: float32 [4096, 1024], P('shard')
- reduce_bias_adjoint: float32 [1024], P('shard')
- first_gain_adjoint: float32 [1024], P('shard')
- first_shift_adjoint: float32 [1024], P('shard')
- second_gain_adjoint: float32 [1024], P('shard')
- second_shift_adjoint: float32 [1024], P('shard')
- attention_scale_adjoint: float32 [1024], P('shard')
- feedforward_scale_adjoint: float32 [1024], P('shard')
The draws below stay inside these ranges and needn't reach their ends.
All inputs are finite; a program needn't handle non-finite values.
Results may differ from the reference program's by a relative error of at most 0.024.
Values may be sent and summed in bfloat16 or wider, within the bound.
No kernel may reach another device: no remote copies, remote signals or barrier semaphores. Data moves between devices by JAX's collectives and lax.ppermute only.
A program may use at most 128 MiB of HBM per device.

```python
import math
import jax
import jax.numpy as jnp
from jax import lax

D = 1024
HEADS = 16
HEAD_DIM = 64
FF = 4096
SEQ = 1024
BATCH = 16


def steps_of(key, extent, shards, low, top_value):
    level, own = 1.0, jax.random.fold_in(key, 6)
    for dim, parts in shards:
        steps = jnp.exp(jax.random.uniform(jax.random.fold_in(own, dim), (parts,), jnp.float32, low / len(shards), top_value / len(shards)))
        level = level * jnp.repeat(steps, extent[dim] // parts).reshape([-1 if axis == dim else 1 for axis in range(len(extent))])
    return level


def normal_values(key, extent, deviation, most, cuts=(), held_as=jnp.bfloat16):
    values = jax.random.normal(key, extent, jnp.float32) * deviation
    if len(cuts) > 0:
        values = steps_of(key, extent, cuts, -0.22, 0.18) * values
    return jnp.clip(values, min=-most, max=most).astype(held_as)


def setup_inputs(seed: int = 0) -> dict:
    seeds = jax.random.split(jax.random.key(seed), 17)
    tokens = normal_values(seeds[0], (BATCH, SEQ, D), 1.0, 6.0, ((0, 16), (1, 8)))
    input_weight = normal_values(seeds[1], (D, 3 * D), D ** -0.5, 0.1875, ((0, 8),))
    query_value_bias = normal_values(seeds[2], (2 * D,), 0.5, 3.0, ((0, 8),))
    output_weight = normal_values(seeds[3], (D, D), 2 ** -0.5, 4.0, ((0, 8),))
    output_bias = normal_values(seeds[4], (D,), 0.5, 3.0, ((0, 8),))
    expand_weight = normal_values(seeds[5], (D, FF), D ** -0.5, 0.1875, ((0, 8),))
    expand_bias = normal_values(seeds[6], (FF,), 0.5, 3.0, ((0, 8),))
    reduce_weight = normal_values(seeds[7], (FF, D), FF ** -0.5, 0.09375, ((0, 8),))
    reduce_bias = normal_values(seeds[8], (D,), 0.5, 3.0, ((0, 8),))
    first_gain = jnp.clip(1.0 + 0.1 * jax.random.normal(seeds[9], (D,), jnp.float32), 0.5, 1.5).astype(jnp.bfloat16)
    first_shift = normal_values(seeds[10], (D,), 0.5, 3.0, ((0, 8),))
    second_gain = jnp.clip(1.0 + 0.1 * jax.random.normal(seeds[11], (D,), jnp.float32), 0.5, 1.5).astype(jnp.bfloat16)
    second_shift = normal_values(seeds[12], (D,), 0.5, 3.0, ((0, 8),))
    attention_scale = jnp.clip(jnp.exp(math.log(2.0) - 1.3862944 * jax.random.uniform(seeds[13], (D,), jnp.float32) ** steps_of(seeds[13], (D,), ((0, 8),), -0.2, 0.2)), 0.5, 2.0).astype(jnp.bfloat16)
    feedforward_scale = jnp.clip(jnp.exp(math.log(2.0) - 1.3862944 * jax.random.uniform(seeds[14], (D,), jnp.float32) ** steps_of(seeds[14], (D,), ((0, 8),), -0.2, 0.2)), 0.5, 2.0).astype(jnp.bfloat16)
    cotangent = normal_values(seeds[15], (BATCH, SEQ, D), 1.0, 6.0, ((0, 16), (1, 8)))
    return {"tokens": tokens, "input_weight": input_weight, "query_value_bias": query_value_bias, "output_weight": output_weight, "output_bias": output_bias, "expand_weight": expand_weight, "expand_bias": expand_bias, "reduce_weight": reduce_weight, "reduce_bias": reduce_bias, "first_gain": first_gain, "first_shift": first_shift, "second_gain": second_gain, "second_shift": second_shift, "attention_scale": attention_scale, "feedforward_scale": feedforward_scale, "cotangent": cotangent}


@jax.custom_vjp
def low(v):
    return lax.optimization_barrier(v.astype(jnp.bfloat16)).astype(jnp.float32)

@jax.custom_vjp
def low_back(v):
    return v

def low_keep(v):
    return (low(v), None)

def low_pass(kept, grad):
    return (grad,)

def back_keep(v):
    return (v, None)

def back_low(kept, grad):
    return (low(grad),)
low.defvjp(low_keep, low_pass)
low_back.defvjp(back_keep, back_low)
epsilon = 1e-06
highest = lax.Precision.HIGHEST

def layer_norm(values, gain, shift):
    mean = lax.optimization_barrier(jnp.mean(values, axis=-1, keepdims=True))
    centred = values - mean
    variance = lax.optimization_barrier(jnp.mean(centred * centred, axis=-1, keepdims=True))
    return centred * lax.rsqrt(variance + epsilon) * gain + shift

def block(image, input_weight, query_value_bias, output_weight, output_bias, expand_weight, expand_bias, reduce_weight, reduce_bias, first_gain, first_shift, second_gain, second_shift, attention_scale, feedforward_scale):
    length = image.shape[0]
    scaling = HEAD_DIM ** (-0.5)
    hidden = low(layer_norm(image, first_gain, first_shift))
    zero_keys = jnp.zeros_like(query_value_bias[:D])
    bias = jnp.concatenate([query_value_bias[:D], zero_keys, query_value_bias[D:]])
    mixed = low(low_back(jnp.dot(hidden, input_weight, precision=highest) + bias))
    query = mixed[:, :D].reshape(length, HEADS, HEAD_DIM)
    keys = mixed[:, D:2 * D].reshape(length, HEADS, HEAD_DIM)
    values = mixed[:, 2 * D:].reshape(length, HEADS, HEAD_DIM)
    scores = low_back(jnp.einsum('qhd,khd->hqk', query, keys, precision=highest) * scaling)
    lse = jax.nn.logsumexp(scores, axis=-1, keepdims=True)
    probs = low(jnp.exp(scores - lse))
    attended = jnp.einsum('hqk,khd->qhd', probs, values, precision=highest).reshape(length, D)
    attended = low(low_back(attended))
    branch = low_back(jnp.dot(attended, output_weight, precision=highest) + output_bias)
    after = image + attention_scale * branch
    second = low(layer_norm(after, second_gain, second_shift))
    pre = low_back(jnp.dot(second, expand_weight, precision=highest) + expand_bias)
    act = low(jax.nn.gelu(pre, approximate=False))
    down = low_back(jnp.dot(act, reduce_weight, precision=highest) + reduce_bias)
    return after + feedforward_scale * down

def reference(tokens, input_weight, query_value_bias, output_weight, output_bias, expand_weight, expand_bias, reduce_weight, reduce_bias, first_gain, first_shift, second_gain, second_shift, attention_scale, feedforward_scale, cotangent):
    params = tuple((p.astype(jnp.float32) for p in (input_weight, query_value_bias, output_weight, output_bias, expand_weight, expand_bias, reduce_weight, reduce_bias, first_gain, first_shift, second_gain, second_shift, attention_scale, feedforward_scale)))

    def one_image(totals, pair):
        image, upstream = pair
        result, pull = jax.vjp(block, image.astype(jnp.float32), *params)
        adjoints = pull(upstream.astype(jnp.float32))
        totals = tuple((t + a for t, a in zip(totals, adjoints[1:])))
        return (totals, (result.astype(jnp.bfloat16), adjoints[0].astype(jnp.bfloat16)))
    start = tuple((jnp.zeros_like(p) for p in params))
    totals, (layer_output, tokens_adjoint) = lax.scan(one_image, start, (tokens, cotangent))
    return (layer_output, tokens_adjoint, totals[0], totals[1], totals[2], totals[3], totals[4], totals[5], totals[6], totals[7], totals[8], totals[9], totals[10], totals[11], totals[12], totals[13])
```

```python
import jax
import jax.numpy as jnp
from jax import lax
from jax.sharding import Mesh, PartitionSpec as P

HEAD_DIM = 64
EPSILON = 1e-06
SHARD = ("z", "yl")
REP = ("yh", "x", "core")
NZ, NX = 4, 4
f32 = jnp.float32
bf16 = jnp.bfloat16


def normalised(values):
    mean = jnp.mean(values, axis=-1, keepdims=True)
    centred = values - mean
    variance = jnp.mean(centred * centred, axis=-1, keepdims=True)
    return centred * lax.rsqrt(variance + EPSILON)


def layer_norm(values, gain, shift):
    return normalised(values) * gain + shift


def exact_gelu(values):
    return jax.nn.gelu(values, approximate=False)


def times(left, right):
    return jnp.dot(left, right, preferred_element_type=f32)


def against(left, right):
    return lax.dot_general(left, right, (((1,), (1,)), ((), ())), preferred_element_type=f32)


def across(left, right):
    return lax.dot_general(left, right, (((0,), (0,)), ((), ())), preferred_element_type=f32)


SWAP = [(0, 1), (1, 0)]


def from_ahead(block, axis, n, k):
    return lax.ppermute(block, axis, [((i + k) % n, i) for i in range(n)])


def to_ahead(block, axis, n, k):
    return lax.ppermute(block, axis, [(i, (i + k) % n) for i in range(n)])


def gather_shard(block):
    other = lax.ppermute(block, "yl", SWAP)
    near = [block] + [from_ahead(block, "z", NZ, k) for k in range(1, NZ)]
    far = [other] + [from_ahead(other, "z", NZ, k) for k in range(1, NZ)]
    return near + far


def scatter_sum_shard(parts, rows):
    def along_z(base):
        total = parts[base * rows : (base + 1) * rows].astype(f32)
        for k in range(1, NZ):
            sent = parts[(base + k) * rows : (base + k + 1) * rows]
            total = total + to_ahead(sent, "z", NZ, k).astype(f32)
        return total

    other = lax.ppermute(along_z(NZ).astype(bf16), "yl", SWAP)
    return along_z(0) + other.astype(f32)


def pick(array, index, axis=0):
    return lax.dynamic_index_in_dim(array, index, axis, keepdims=False)


def reduce_rep(parts, core, x):
    parts = parts.astype(bf16)
    mine = pick(parts, core).astype(f32)
    total = (mine + lax.ppermute(pick(parts, 1 - core), "core", SWAP).astype(f32)).astype(bf16)
    mine = pick(total, x).astype(f32)
    for k in range(1, NX):
        mine = mine + to_ahead(pick(total, (x + k) % NX), "x", NX, k).astype(f32)
    mine = mine.astype(bf16)
    other = lax.ppermute(mine, "yh", SWAP)
    return (mine.astype(f32) + other.astype(f32)).astype(bf16)


def spread_rep(block):
    return lax.all_gather(block, ("core", "x"), axis=0, tiled=True)


def attend_forward(query, key, value, scaling):
    scores = jnp.einsum("qhd,khd->hqk", query, key, preferred_element_type=f32) * scaling
    lse = jax.nn.logsumexp(scores, axis=-1, keepdims=True)
    probs = jnp.exp(scores - lse).astype(bf16)
    attended = jnp.einsum("hqk,khd->qhd", probs, value, preferred_element_type=f32)
    return attended, lse


def attend_backward(query, key, value, lse, grad, scaling):
    scores = jnp.einsum("qhd,khd->hqk", query, key, preferred_element_type=f32) * scaling
    weights = jnp.exp(scores - lse)
    probs = weights.astype(bf16)
    prob_adj = jnp.einsum("qhd,khd->hqk", grad, value, preferred_element_type=f32)
    delta = jnp.sum(weights * prob_adj, axis=-1, keepdims=True)
    score_adj = (weights * (prob_adj - delta)).astype(bf16)
    query_adj = jnp.einsum("hqk,khd->qhd", score_adj, key, preferred_element_type=f32) * scaling
    key_adj = jnp.einsum("hqk,qhd->khd", score_adj, query, preferred_element_type=f32) * scaling
    value_adj = jnp.einsum("hqk,qhd->khd", probs, grad, preferred_element_type=f32)
    return query_adj, key_adj, value_adj


def shards(
    tokens,
    input_weight,
    query_value_bias,
    output_weight,
    output_bias,
    expand_weight,
    expand_bias,
    reduce_weight,
    reduce_bias,
    first_gain,
    first_shift,
    second_gain,
    second_shift,
    attention_scale,
    feedforward_scale,
    cotangent,
):
    _, rows, width = tokens.shape
    units = reduce_weight.shape[0]
    part = output_weight.shape[0]
    heads = part // HEAD_DIM
    group = 8
    length = group * rows
    scaling = HEAD_DIM ** (-0.5)
    z, yl = lax.axis_index("z"), lax.axis_index("yl")
    x, core = lax.axis_index("x"), lax.axis_index("core")
    me = z * 2 + yl

    w = input_weight.reshape(part, 3, group, part)
    in_w = lax.all_to_all(w, SHARD, split_axis=2, concat_axis=0, tiled=True).reshape(width, 3 * part)
    w = expand_weight.reshape(part, group, units)
    up_w = lax.all_to_all(w, SHARD, split_axis=1, concat_axis=0, tiled=True).reshape(width, units)

    small = jnp.concatenate(
        [
            query_value_bias,
            output_bias,
            reduce_bias,
            first_gain,
            first_shift,
            second_gain,
            second_shift,
            attention_scale,
            feedforward_scale,
        ]
    )
    extra = 8
    small = jnp.pad(small, (0, extra * width - small.shape[0])).reshape(extra, width)
    own = tokens[0]
    blocks = gather_shard(jnp.concatenate([own, small], axis=0))
    all_tokens = jnp.concatenate([b[:rows] for b in blocks], axis=0).astype(f32)
    smalls = jnp.stack([b[rows : rows + 2].reshape(2 * width) for b in blocks])
    zz, yy = jnp.arange(group) // 2, jnp.arange(group) % 2
    place = ((yy - yl) % 2) * NZ + (zz - z) % NZ
    chosen = (place[:, None] == jnp.arange(group)[None, :]).astype(bf16)
    smalls = times(chosen, smalls)
    pair_bias = smalls[:, : 2 * part].reshape(2 * width)
    out_bias, down_bias, gain_one, shift_one, gain_two, shift_two, scale_one, scale_two = [
        smalls[:, (2 + j) * part : (3 + j) * part].reshape(width) for j in range(8)
    ]
    bias = jnp.concatenate(
        [
            lax.dynamic_slice(pair_bias, (me * part,), (part,)),
            jnp.zeros((part,), f32),
            lax.dynamic_slice(pair_bias, (width + me * part,), (part,)),
        ]
    )
    upstreams = jnp.concatenate(gather_shard(cotangent[0]), axis=0).astype(f32)

    local = own.astype(f32)
    normal_one = normalised(all_tokens)
    hidden = (normal_one * gain_one + shift_one).astype(bf16)
    mixed = (times(hidden, in_w) + bias).astype(bf16)
    query, key, value = [
        mixed[:, j * part : (j + 1) * part].reshape(length, heads, HEAD_DIM) for j in range(3)
    ]
    attended, lse = attend_forward(query, key, value, scaling)
    attended = attended.reshape(length, part).astype(bf16)
    branch = scatter_sum_shard(times(attended, output_weight).astype(bf16), rows) + out_bias
    after = local + scale_one * branch

    second_own = layer_norm(after, gain_two, shift_two).astype(bf16)
    second = jnp.concatenate(gather_shard(second_own), axis=0)
    pre = times(second, up_w) + expand_bias.astype(f32)
    act = exact_gelu(pre).astype(bf16)

    down_adj = (scale_two * upstreams).astype(bf16)
    act_adj = against(down_adj, reduce_weight)
    _, gelu_pull = jax.vjp(exact_gelu, pre)
    pre_adj = gelu_pull(act_adj)[0].astype(bf16)
    second_adj = scatter_sum_shard(against(pre_adj, up_w).astype(bf16), rows)
    up_bias_adj = jnp.sum(pre_adj.astype(f32), axis=0)
    down_weight_adj = across(act, down_adj)
    up_weight_adj = across(second, pre_adj)

    upstream = cotangent[0].astype(f32)
    _, norm_pull = jax.vjp(layer_norm, after, gain_two, shift_two)
    after_inner, gain_two_adj, shift_two_adj = norm_pull(second_adj)
    after_adj = upstream + after_inner
    branch_adj_own = (scale_one * after_adj).astype(bf16)
    scale_one_adj = jnp.sum(after_adj * branch, axis=0)
    out_bias_adj = jnp.sum(branch_adj_own.astype(f32), axis=0)
    branch_adj = jnp.concatenate(gather_shard(branch_adj_own), axis=0)

    down = scatter_sum_shard(times(act, reduce_weight).astype(bf16), rows) + down_bias
    layer_output = (after + scale_two * down).astype(bf16)
    scale_two_adj = jnp.sum(upstream * down, axis=0)
    down_bias_adj = jnp.sum((scale_two * upstream).astype(bf16).astype(f32), axis=0)

    attended_adj = against(branch_adj, output_weight).astype(bf16)
    out_weight_adj = across(attended, branch_adj)
    grad = attended_adj.reshape(length, heads, HEAD_DIM)
    pieces = attend_backward(query, key, value, lse, grad, scaling)
    mixed_adj = jnp.concatenate([p.reshape(length, part) for p in pieces], axis=1).astype(bf16)
    hidden_part = against(mixed_adj, in_w)
    hidden_adj = scatter_sum_shard(hidden_part.astype(bf16), rows)
    _, first_pull = jax.vjp(lambda v: normalised(v) * gain_one, local)
    tokens_adjoint = (after_adj + first_pull(hidden_adj)[0]).astype(bf16)
    gain_one_adj = jnp.sum(hidden_part * normal_one, axis=0)
    shift_one_adj = jnp.sum(hidden_part, axis=0)
    in_weight_adj = across(hidden, mixed_adj)
    sums = jnp.sum(mixed_adj.astype(f32), axis=0)

    piece = part // 8

    def by_rows(array, kinds):
        columns = array.shape[-1]
        array = array.reshape(group, 2, NX, piece, columns)
        array = reduce_rep(array.transpose(1, 2, 0, 3, 4), core, x)
        array = lax.all_to_all(array, SHARD, split_axis=0, concat_axis=0, tiled=True)
        array = array.reshape(group, piece, kinds, columns // kinds).transpose(1, 2, 0, 3)
        array = array.reshape(piece, group * columns)
        return spread_rep(array).astype(f32)

    def in_place(array):
        n, columns = array.shape
        array = reduce_rep(array.reshape(2, NX, n // 8, columns), core, x)
        return spread_rep(array).astype(f32)

    down_weight_adj = in_place(down_weight_adj)
    up_weight_adj = by_rows(up_weight_adj, 1)
    out_weight_adj = in_place(out_weight_adj)
    in_weight_adj = by_rows(in_weight_adj, 3)

    pair_sums = jnp.zeros((2 * width,), f32)
    pair_sums = lax.dynamic_update_slice(pair_sums, sums[:part], (me * part,))
    pair_sums = lax.dynamic_update_slice(pair_sums, sums[2 * part :], (width + me * part,))
    vectors = [
        out_bias_adj,
        down_bias_adj,
        gain_one_adj,
        shift_one_adj,
        gain_two_adj,
        shift_two_adj,
        scale_one_adj,
        scale_two_adj,
    ]
    ups = jnp.zeros((group, units), f32)
    ups = lax.dynamic_update_slice(ups, up_bias_adj[None], (me, 0))
    packed = jnp.concatenate(
        [pair_sums.reshape(group, 2 * part), ups] + [v.reshape(group, part) for v in vectors], axis=1
    )
    count = packed.shape[1]
    packed = jnp.pad(packed, ((0, 0), (0, 2 * width - count))).reshape(group, 2, NX, 2 * width // 8)
    packed = reduce_rep(packed.transpose(1, 2, 0, 3), core, x)
    packed = lax.all_to_all(packed, SHARD, split_axis=0, concat_axis=0, tiled=True)
    packed = jnp.sum(packed.astype(f32), axis=0).astype(bf16)
    packed = spread_rep(packed).astype(f32)
    pair_sums = packed[: 2 * part]
    ups = packed[2 * part : 2 * part + units]
    at = 2 * part + units
    vectors = [packed[at + j * part : at + (j + 1) * part] for j in range(8)]

    return (
        layer_output[None],
        tokens_adjoint[None],
        in_weight_adj,
        pair_sums,
        out_weight_adj,
        vectors[0],
        up_weight_adj,
        ups,
        down_weight_adj,
        vectors[1],
        *vectors[2:],
    )


def solution(mesh):
    fine = Mesh(mesh.devices.reshape(2, NX, 2, NZ, 2), REP + SHARD)
    rows = P(REP, SHARD, None)
    matrix, vector = P(SHARD, None), P(SHARD)
    placed = (
        rows,
        matrix,
        vector,
        matrix,
        vector,
        matrix,
        vector,
        matrix,
        *[vector] * 7,
        rows,
    )
    return jax.shard_map(
        shards,
        mesh=fine,
        in_specs=placed,
        out_specs=(
            rows,
            rows,
            matrix,
            vector,
            matrix,
            vector,
            matrix,
            vector,
            matrix,
            *[vector] * 7,
        ),
        check_vma=False,
    )
```

```python
import functools

import jax
import jax.numpy as jnp
from jax import lax
from jax.experimental import pallas as pl
from jax.experimental.pallas import tpu as pltpu
from jax.sharding import Mesh, PartitionSpec as P

HEAD_DIM = 64
EPSILON = 1e-06
SHARD = ("z", "yl")
REP = ("yh", "x", "core")
NZ, NX = 4, 4
f32 = jnp.float32
bf16 = jnp.bfloat16


def normalised(values):
    mean = jnp.mean(values, axis=-1, keepdims=True)
    centred = values - mean
    variance = jnp.mean(centred * centred, axis=-1, keepdims=True)
    return centred * lax.rsqrt(variance + EPSILON)


def layer_norm(values, gain, shift):
    return normalised(values) * gain + shift


def exact_gelu(values):
    return jax.nn.gelu(values, approximate=False)


def times(left, right):
    return jnp.dot(left, right, preferred_element_type=f32)


def against(left, right):
    return lax.dot_general(left, right, (((1,), (1,)), ((), ())), preferred_element_type=f32)


def across(left, right):
    return lax.dot_general(left, right, (((0,), (0,)), ((), ())), preferred_element_type=f32)


SWAP = [(0, 1), (1, 0)]


def swap(block, axis):
    return lax.ppermute(block, axis, SWAP)


def trade(parts, axes):
    return lax.all_to_all(parts, axes, split_axis=0, concat_axis=0, tiled=True)


def gather(block, axes, n):
    return trade(jnp.broadcast_to(block[None], (n, *block.shape)), axes)


def pick(array, index, axis=0):
    return lax.dynamic_index_in_dim(array, index, axis, keepdims=False)


def both_cores(half, axis):
    other = swap(half, "core")
    first = lax.axis_index("core") == 0
    return jnp.concatenate([jnp.where(first, half, other), jnp.where(first, other, half)], axis=axis)


def ahead(block, axis, n, k):
    return lax.ppermute(block, axis, [((i + k) % n, i) for i in range(n)])


def give(block, axis, n, k):
    return lax.ppermute(block, axis, [(i, (i + k) % n) for i in range(n)])


def gather_x(block):
    return jnp.concatenate([block] + [ahead(block, "x", NX, k) for k in range(1, NX)], axis=0)


def return_x(parts):
    sent = [give(parts[k], "x", NX, k) for k in range(1, NX)]
    return parts[0].astype(f32) + sum(p.astype(f32) for p in sent)


def gather_shard(block):
    other = swap(block, "yl")
    low = lax.axis_index("yl") == 0
    column = jnp.stack([jnp.where(low, block, other), jnp.where(low, other, block)])
    z = lax.axis_index("z")
    out = jnp.zeros((2, NZ, *block.shape), block.dtype)
    for k in range(NZ):
        arrived = ahead(column, "z", NZ, k) if k else column
        out = lax.dynamic_update_slice_in_dim(out, arrived[:, None], (z + k) % NZ, 1)
    return out


def sum_shard(parts):
    z, yl = lax.axis_index("z"), lax.axis_index("yl")
    column = pick(parts, z).astype(f32)
    for k in range(1, NZ):
        column = column + give(pick(parts, (z + k) % NZ), "z", NZ, k).astype(f32)
    column = column.astype(bf16)
    return (pick(column, yl).astype(f32) + swap(pick(column, 1 - yl), "yl").astype(f32)).astype(bf16)


def whole_x(block):
    x = lax.axis_index("x")
    ring = jnp.zeros((NX, *block.shape), block.dtype)
    for k in range(NX):
        arrived = ahead(block, "x", NX, k) if k else block
        ring = lax.dynamic_update_slice_in_dim(ring, arrived[None], (x + k) % NX, 0)
    return ring


def place(vector, offset, shape):
    row, column = divmod(offset, shape[1])
    size = vector.shape[0]
    return jnp.pad(vector.reshape(1, size), ((row, shape[0] - row - 1), (column, shape[1] - column - size)))


def after_that(value, earlier):
    return lax.optimization_barrier((value, earlier))[0]


def total(parts):
    return jnp.sum(parts.astype(f32), axis=0)


BLOCK = 256


def head_parts(mixed_ref, head, part):
    return [
        mixed_ref[:, j * part + head * HEAD_DIM : j * part + (head + 1) * HEAD_DIM] for j in range(3)
    ]


def forward_kernel(scaling, mixed_ref, attended_ref, lse_ref):
    length, part = attended_ref.shape
    for head in range(part // HEAD_DIM):
        query, key, value = head_parts(mixed_ref, head, part)
        query = query * jnp.asarray(scaling, bf16)
        value_t = value.T
        for at in range(0, length, BLOCK):
            scores = against(key, query[at : at + BLOCK])
            most = jnp.max(scores, axis=0, keepdims=True)
            weights = jnp.exp(scores - most)
            count = jnp.sum(weights, axis=0, keepdims=True)
            probs = (weights * (1.0 / count)).astype(bf16)
            attended_ref[at : at + BLOCK, head * HEAD_DIM : (head + 1) * HEAD_DIM] = (
                times(value_t, probs).T.astype(bf16)
            )
            lse_ref[head : head + 1, at : at + BLOCK] = most + jnp.log(count)


def backward_kernel(scaling, mixed_ref, lse_ref, grad_ref, out_ref):
    length, part = grad_ref.shape
    for head in range(part // HEAD_DIM):
        query, key, value = head_parts(mixed_ref, head, part)
        query = query * jnp.asarray(scaling, bf16)
        key_t = key.T
        columns = slice(head * HEAD_DIM, (head + 1) * HEAD_DIM)
        key_adj = jnp.zeros((length, HEAD_DIM), f32)
        value_adj = jnp.zeros((length, HEAD_DIM), f32)
        for at in range(0, length, BLOCK):
            rows = slice(at, at + BLOCK)
            grad = grad_ref[rows, columns]
            scores = against(key, query[rows])
            weights = jnp.exp(scores - lse_ref[head : head + 1, rows])
            prob_adj = against(value, grad)
            delta = jnp.sum(weights * prob_adj, axis=0, keepdims=True)
            score_adj = (weights * (prob_adj - delta)).astype(bf16)
            key_adj += times(score_adj, query[rows])
            value_adj += times(weights.astype(bf16), grad)
            out_ref[rows, columns] = (times(key_t, score_adj) * scaling).T.astype(bf16)
        out_ref[:, part + columns.start : part + columns.stop] = key_adj.astype(bf16)
        out_ref[:, 2 * part + columns.start : 2 * part + columns.stop] = value_adj.astype(bf16)


def attend_forward(mixed, scaling):
    length, part = mixed.shape[0], mixed.shape[1] // 3
    pairs = part * length * length
    return pl.pallas_call(
        functools.partial(forward_kernel, scaling),
        out_shape=(
            jax.ShapeDtypeStruct((length, part), bf16),
            jax.ShapeDtypeStruct((8, length), f32),
        ),
        compiler_params=pltpu.CompilerParams(vmem_limit_bytes=40 * 2**20),
        cost_estimate=pl.CostEstimate(
            flops=16 * pairs, bytes_accessed=8 * part * length, transcendentals=pairs // HEAD_DIM
        ),
    )(mixed)


def attend_backward(mixed, lse, grad, scaling):
    length, part = grad.shape
    pairs = part * length * length
    return pl.pallas_call(
        functools.partial(backward_kernel, scaling),
        out_shape=jax.ShapeDtypeStruct(mixed.shape, bf16),
        compiler_params=pltpu.CompilerParams(vmem_limit_bytes=40 * 2**20),
        cost_estimate=pl.CostEstimate(
            flops=40 * pairs, bytes_accessed=16 * part * length, transcendentals=pairs // HEAD_DIM
        ),
    )(mixed, lse, grad)


def shards(
    tokens,
    input_weight,
    query_value_bias,
    output_weight,
    output_bias,
    expand_weight,
    expand_bias,
    reduce_weight,
    reduce_bias,
    first_gain,
    first_shift,
    second_gain,
    second_shift,
    attention_scale,
    feedforward_scale,
    cotangent,
):
    _, rows, width = tokens.shape
    units = reduce_weight.shape[0]
    part = output_weight.shape[0]
    group = 8
    length = group * rows
    half = part // 2
    scaling = HEAD_DIM ** (-0.5)
    me = lax.axis_index("z") * 2 + lax.axis_index("yl")
    x, core = lax.axis_index("x"), lax.axis_index("core")

    own = tokens[0]
    extra = 8
    offset, small = 0, 0
    for vector in (
        query_value_bias,
        output_bias,
        reduce_bias,
        first_gain,
        first_shift,
        second_gain,
        second_shift,
        attention_scale,
        feedforward_scale,
        expand_bias,
    ):
        small = small + place(vector, offset, (extra, width))
        offset += vector.shape[0]
    band = part // 8
    w = input_weight.reshape(8, band, 3, group, part).transpose(3, 2, 1, 0, 4).reshape(group, 3 * band, width)
    here = jnp.concatenate([own, small], axis=0)
    blocks = jnp.concatenate([jnp.broadcast_to(here[None], (group, *here.shape)), w], axis=1)
    blocks = trade(blocks, SHARD)
    all_tokens = blocks[:, :rows].reshape(length, width).astype(f32)
    smalls = blocks[:, rows : rows + 2].reshape(group, 2 * width).astype(f32)
    in_w = blocks[:, rows + extra :].reshape(group, 3, band, 8, part).transpose(0, 3, 2, 1, 4)
    in_w = in_w.reshape(width, 3 * part)
    pair_bias = smalls[:, : 2 * part].reshape(2 * width)
    out_bias, down_bias, gain_one, shift_one, gain_two, shift_two, scale_one, scale_two = [
        smalls[:, (2 + j) * part : (3 + j) * part].reshape(width) for j in range(8)
    ]
    at = 10 * part
    up_bias = pick(smalls[:, at : at + units].reshape(group, NX, part), x, 1).reshape(width)
    bias = jnp.concatenate(
        [
            lax.dynamic_slice(pair_bias, (me * part,), (part,)),
            jnp.zeros((part,), f32),
            lax.dynamic_slice(pair_bias, (width + me * part,), (part,)),
        ]
    )

    piece = part // 8
    up_half = lax.dynamic_slice_in_dim(expand_weight, core * half, half, 0)
    up_half = pick(up_half.reshape(half, group, NX, part), x, 2).reshape(half, width)
    down_half = lax.dynamic_slice_in_dim(reduce_weight, x * part + core * half, half, 0)
    out_piece = lax.dynamic_slice_in_dim(output_weight, core * half + x * piece, piece, 0)
    w = gather_shard(jnp.concatenate([up_half, down_half, out_piece], axis=0))
    w = w.transpose(1, 0, 2, 3).reshape(group, 2 * half + piece, width)
    out_w = whole_x(w[:, 2 * half :]).transpose(1, 0, 2, 3).reshape(group, half, width)
    out_w = both_cores(out_w, 1).reshape(width, width)
    up_w = both_cores(w[:, :half], 1).reshape(width, width)
    down_w = both_cores(w[:, half : 2 * half], 1).reshape(width, width)
    upstreams = gather_x(cotangent[0]).astype(f32)

    local = own.astype(f32)
    normal_one = normalised(all_tokens)
    hidden = (normal_one * gain_one + shift_one).astype(bf16)
    mixed = (times(hidden, in_w) + bias).astype(bf16)
    attended, lse = attend_forward(mixed, scaling)
    attended = trade(attended.reshape(group, rows, part), SHARD)
    attended = attended.transpose(1, 0, 2).reshape(rows, width)
    branch = times(attended, out_w) + out_bias
    after = local + scale_one * branch

    second_own = layer_norm(after, gain_two, shift_two).astype(bf16)
    second = gather_x(second_own)
    down_adj = (scale_two * upstreams).astype(bf16)

    pre = times(second, up_w) + up_bias
    act, gelu_pull = jax.vjp(exact_gelu, pre)
    act = act.astype(bf16)
    pre_adj = gelu_pull(against(down_adj, down_w))[0].astype(bf16)
    second_adj = return_x(against(pre_adj, up_w).astype(bf16).reshape(NX, rows, width))

    def add(mine, other, axis):
        return (mine.astype(f32) + swap(other.astype(bf16), axis).astype(f32)).astype(bf16)

    def core_sum(array):
        return add(pick(array, core, 1), pick(array, 1 - core, 1), "core")

    pair = jnp.stack(
        [
            core_sum(g.astype(bf16).reshape(group, 2, half, width))
            for g in (across(act, down_adj), across(second, pre_adj))
        ],
        axis=1,
    )
    second_adj, pair = lax.optimization_barrier((second_adj, pair))

    upstream = cotangent[0].astype(f32)
    _, norm_pull = jax.vjp(layer_norm, after, gain_two, shift_two)
    after_inner, gain_two_adj, shift_two_adj = norm_pull(second_adj)
    after_adj = upstream + after_inner
    branch_adj = (scale_one * after_adj).astype(bf16)

    attended_adj = against(branch_adj, out_w).astype(bf16)
    attended_adj = trade(attended_adj.reshape(rows, group, part).transpose(1, 0, 2), SHARD)
    mixed_adj = attend_backward(mixed, lse, attended_adj.reshape(length, part), scaling)
    in_weight_adj = across(hidden, mixed_adj)
    hidden_part = against(mixed_adj, in_w)
    hidden_adj = total(trade(hidden_part.astype(bf16).reshape(group, rows, width), SHARD))
    _, first_pull = jax.vjp(lambda v: normalised(v) * gain_one, local)
    tokens_adjoint = (after_adj + first_pull(hidden_adj)[0]).astype(bf16)

    down_part = times(act, down_w).astype(bf16)
    down = return_x(after_that(down_part, second_adj).reshape(NX, rows, width)) + down_bias
    layer_output = (after + scale_two * down).astype(bf16)

    pair = sum_shard(pair.reshape(NZ, 2, part, width))
    pair = whole_x(add(pair, pair, "yh"))
    pair = both_cores(pair.reshape(NX, 2, half, width), 2)
    reduce_weight_adj = pair[:, 0].reshape(units, width).astype(f32)
    expand_weight_adj = pair[:, 1].reshape(NX, part, group, part).transpose(1, 2, 0, 3)
    expand_weight_adj = expand_weight_adj.reshape(part, group * units).astype(f32)

    def chip_row_sum(array):
        array = core_sum(array.reshape(group, 2, NX, piece, array.shape[-1]))
        return return_x([pick(array, (x + k) % NX, 1) for k in range(NX)]).astype(bf16)

    out_sum = chip_row_sum(across(attended, branch_adj).astype(bf16))

    sums = jnp.sum(mixed_adj.astype(f32), axis=0)
    pairs = jnp.zeros((width,), f32)
    pairs = lax.dynamic_update_slice(pairs, sums[:part], ((me // 2) * part,))
    pairs = lax.dynamic_update_slice(pairs, sums[2 * part :], (width // 2 + (me // 2) * part,))
    even = (me % 2 == 0).astype(f32)
    up_sums = jnp.sum(pre_adj.astype(f32), axis=0)
    vectors = [
        jnp.sum(branch_adj.astype(f32), axis=0),
        jnp.sum((scale_two * upstream).astype(bf16).astype(f32), axis=0),
        jnp.sum(hidden_part * normal_one, axis=0),
        jnp.sum(hidden_part, axis=0),
        gain_two_adj,
        shift_two_adj,
        jnp.sum(after_adj * branch, axis=0),
        jnp.sum(upstream * down, axis=0),
        pairs * even,
        pairs * (1 - even),
        *[up_sums * (x == j).astype(f32) for j in range(NX)],
    ]
    columns = jnp.stack(vectors).astype(bf16).T
    columns = jnp.pad(columns, ((0, 0), (0, part - columns.shape[1])))
    last = chip_row_sum(jnp.concatenate([in_weight_adj.astype(bf16), columns], axis=1))
    last = jnp.concatenate([last, out_sum], axis=2)
    last = trade(add(last, last, "yh"), SHARD)
    matrix = last[:, :, : 3 * part].reshape(group, piece, 3, part).transpose(1, 2, 0, 3).reshape(piece, 3 * width)
    sums = total(last[:, :, 3 * part :]).astype(bf16)
    last = whole_x(jnp.concatenate([matrix, sums], axis=1))
    last = both_cores(last.reshape(half, 4 * width + part), 0).astype(f32)
    output_weight_adj = last[:, 3 * width + part :]
    input_weight_adj = last[:, : 3 * width]
    vectors = last[:, 3 * width : 3 * width + 14].T

    return (
        layer_output[None],
        tokens_adjoint[None],
        input_weight_adj,
        vectors[8:10].reshape(2 * part),
        output_weight_adj,
        vectors[0],
        expand_weight_adj,
        vectors[10:14].reshape(units),
        reduce_weight_adj,
        vectors[1],
        *[vectors[j] for j in range(2, 8)],
    )


def solution(mesh):
    fine = Mesh(mesh.devices.reshape(2, NX, 2, NZ, 2), REP + SHARD)
    rows = P(REP, SHARD, None)
    matrix, vector = P(SHARD, None), P(SHARD)
    placed = (
        rows,
        matrix,
        vector,
        matrix,
        vector,
        matrix,
        vector,
        matrix,
        *[vector] * 7,
        rows,
    )
    return jax.shard_map(
        shards,
        mesh=fine,
        in_specs=placed,
        out_specs=(
            rows,
            rows,
            matrix,
            vector,
            matrix,
            vector,
            matrix,
            vector,
            matrix,
            *[vector] * 7,
        ),
        check_vma=False,
    )
```

```python
import functools

import jax
import jax.numpy as jnp
from jax import lax
from jax.experimental import pallas as pl
from jax.experimental.pallas import tpu as pltpu
from jax.sharding import Mesh, PartitionSpec as P

HEAD_DIM = 64
EPSILON = 1e-06
SHARD = ("z", "yl")
REP = ("yh", "x", "core")
NZ, NX = 4, 4
f32 = jnp.float32
bf16 = jnp.bfloat16


def normalised(values):
    mean = jnp.mean(values, axis=-1, keepdims=True)
    centred = values - mean
    variance = jnp.mean(centred * centred, axis=-1, keepdims=True)
    return centred * lax.rsqrt(variance + EPSILON)


def layer_norm(values, gain, shift):
    return normalised(values) * gain + shift


def exact_gelu(values):
    return jax.nn.gelu(values, approximate=False)


def times(left, right):
    return jnp.dot(left, right, preferred_element_type=f32)


def against(left, right):
    return lax.dot_general(left, right, (((1,), (1,)), ((), ())), preferred_element_type=f32)


def across(left, right):
    return lax.dot_general(left, right, (((0,), (0,)), ((), ())), preferred_element_type=f32)


SWAP = [(0, 1), (1, 0)]


def swap(block, axis):
    return lax.ppermute(block, axis, SWAP)


def trade(parts, axes):
    return lax.all_to_all(parts, axes, split_axis=0, concat_axis=0, tiled=True)


def gather(block, axes, n):
    return trade(jnp.broadcast_to(block[None], (n, *block.shape)), axes)


def pick(array, index, axis=0):
    return lax.dynamic_index_in_dim(array, index, axis, keepdims=False)


def both_cores(half, axis):
    other = swap(half, "core")
    first = lax.axis_index("core") == 0
    return jnp.concatenate([jnp.where(first, half, other), jnp.where(first, other, half)], axis=axis)


def ahead(block, axis, n, k):
    return lax.ppermute(block, axis, [((i + k) % n, i) for i in range(n)])


def give(block, axis, n, k):
    return lax.ppermute(block, axis, [(i, (i + k) % n) for i in range(n)])


def gather_x(block):
    return jnp.concatenate([block] + [ahead(block, "x", NX, k) for k in range(1, NX)], axis=0)


def return_x(parts):
    sent = [give(parts[k], "x", NX, k) for k in range(1, NX)]
    return parts[0].astype(f32) + sum(p.astype(f32) for p in sent)


def gather_column(block, other):
    low = lax.axis_index("yl") == 0
    column = jnp.stack([jnp.where(low, block, other), jnp.where(low, other, block)])
    return [column] + [ahead(column, "z", NZ, k) for k in range(1, NZ)]


def send_z(parts):
    z = lax.axis_index("z")
    return [pick(parts, z)] + [give(pick(parts, (z + k) % NZ), "z", NZ, k) for k in range(1, NZ)]


def arrivals(block):
    blocks = [block] + [ahead(block, "x", NX, k) for k in range(1, NX)]
    return blocks + [swap(b, "core") for b in blocks]


def place(vector, offset, shape):
    row, column = divmod(offset, shape[1])
    size = vector.shape[0]
    return jnp.pad(vector.reshape(1, size), ((row, shape[0] - row - 1), (column, shape[1] - column - size)))


def after_that(value, earlier):
    return lax.optimization_barrier((value, earlier))[0]


def total(parts):
    return jnp.sum(parts.astype(f32), axis=0)


VMEM = pl.BlockSpec(memory_space=pltpu.VMEM)


def assemble_kernel(place_ref, *refs):
    columns, outs = refs[:-3], refs[-3:]
    z, core = place_ref[0], place_ref[1]
    half = columns[0].shape[1] // 3
    for j, column in enumerate(columns):
        block, side = j % NZ, core if j < NZ else 1 - core
        for y in range(2):
            first = ((lax.rem(z + block, NZ) * 2 + y) * 2 + side) * half
            rows = pl.ds(pl.multiple_of(first, half), half)
            for out, at in zip(outs, range(0, 3 * half, half)):
                out[rows, :] = column[y, at : at + half, :]


def assemble(columns, z, core, width):
    whole = jax.ShapeDtypeStruct((width, width), bf16)
    return pl.pallas_call(
        assemble_kernel,
        out_shape=(whole, whole, whole),
        in_specs=[pl.BlockSpec(memory_space=pltpu.SMEM)] + [VMEM] * len(columns),
        out_specs=(VMEM, VMEM, VMEM),
        compiler_params=pltpu.CompilerParams(vmem_limit_bytes=32 * 2**20),
        cost_estimate=pl.CostEstimate(flops=0, bytes_accessed=12 * width * width, transcendentals=0),
    )(jnp.stack([z, core]).astype(jnp.int32), *columns)


def finish_kernel(place_ref, *refs):
    pieces, (in_ref, out_ref, vector_ref, scratch) = refs[:-4], refs[-4:]
    x, core = place_ref[0], place_ref[1]
    piece, width, part = pieces[0].shape[0], out_ref.shape[1], scratch.shape[1]
    for j, ref in enumerate(pieces):
        side = core if j < NX else 1 - core
        first = (side * NX + lax.rem(x + j % NX, NX)) * piece
        rows = pl.ds(pl.multiple_of(first, piece), piece)
        in_ref[rows, :] = ref[:, : 3 * width].astype(f32)
        scratch[rows, :] = ref[:, 3 * width : 3 * width + part].astype(f32)
        out_ref[rows, :] = ref[:, 3 * width + part :].astype(f32)
    vector_ref[...] = scratch[...].T


def finish(pieces, x, core, part, width):
    return pl.pallas_call(
        finish_kernel,
        out_shape=(
            jax.ShapeDtypeStruct((part, 3 * width), f32),
            jax.ShapeDtypeStruct((part, width), f32),
            jax.ShapeDtypeStruct((part, part), f32),
        ),
        in_specs=[pl.BlockSpec(memory_space=pltpu.SMEM)] + [VMEM] * len(pieces),
        out_specs=(VMEM, VMEM, VMEM),
        scratch_shapes=[pltpu.VMEM((part, part), f32)],
        compiler_params=pltpu.CompilerParams(vmem_limit_bytes=16 * 2**20),
        cost_estimate=pl.CostEstimate(flops=0, bytes_accessed=24 * part * width, transcendentals=0),
    )(jnp.stack([x, core]).astype(jnp.int32), *pieces)


def finish_pair_kernel(place_ref, *refs):
    pieces, (down_ref, up_ref) = refs[:-2], refs[-2:]
    x, core = place_ref[0], place_ref[1]
    part, width = pieces[0].shape
    half = part // 2
    for j, ref in enumerate(pieces):
        side = core if j < NX else 1 - core
        chip = lax.rem(x + j % NX, NX)
        first = (chip * 2 + side) * half
        down_ref[pl.ds(pl.multiple_of(first, half), half), :] = ref[:half, :].astype(f32)
        rows = pl.ds(pl.multiple_of(side * half, half), half)
        for s in range(width // part):
            at = pl.multiple_of((s * NX + chip) * part, part)
            up_ref[rows, pl.ds(at, part)] = ref[half:, s * part : (s + 1) * part].astype(f32)


def finish_pair(pieces, x, core, part, width):
    return pl.pallas_call(
        finish_pair_kernel,
        out_shape=(
            jax.ShapeDtypeStruct((NX * part, width), f32),
            jax.ShapeDtypeStruct((part, NX * width), f32),
        ),
        in_specs=[pl.BlockSpec(memory_space=pltpu.SMEM)] + [VMEM] * len(pieces),
        out_specs=(VMEM, VMEM),
        compiler_params=pltpu.CompilerParams(vmem_limit_bytes=16 * 2**20),
        cost_estimate=pl.CostEstimate(flops=0, bytes_accessed=48 * part * width, transcendentals=0),
    )(jnp.stack([x, core]).astype(jnp.int32), *pieces)


BLOCK = 256


def head_parts(mixed_ref, head, part):
    return [
        mixed_ref[:, j * part + head * HEAD_DIM : j * part + (head + 1) * HEAD_DIM] for j in range(3)
    ]


def forward_kernel(scaling, mixed_ref, attended_ref, lse_ref):
    length, part = attended_ref.shape
    for head in range(part // HEAD_DIM):
        query, key, value = head_parts(mixed_ref, head, part)
        query = query * jnp.asarray(scaling, bf16)
        value_t = value.T
        for at in range(0, length, BLOCK):
            scores = against(key, query[at : at + BLOCK])
            most = jnp.max(scores, axis=0, keepdims=True)
            weights = jnp.exp(scores - most)
            count = jnp.sum(weights, axis=0, keepdims=True)
            probs = (weights * (1.0 / count)).astype(bf16)
            attended_ref[at : at + BLOCK, head * HEAD_DIM : (head + 1) * HEAD_DIM] = (
                times(value_t, probs).T.astype(bf16)
            )
            lse_ref[head : head + 1, at : at + BLOCK] = most + jnp.log(count)


def backward_kernel(scaling, mixed_ref, lse_ref, grad_ref, out_ref):
    length, part = grad_ref.shape
    for head in range(part // HEAD_DIM):
        query, key, value = head_parts(mixed_ref, head, part)
        query = query * jnp.asarray(scaling, bf16)
        key_t = key.T
        columns = slice(head * HEAD_DIM, (head + 1) * HEAD_DIM)
        key_adj = jnp.zeros((length, HEAD_DIM), f32)
        value_adj = jnp.zeros((length, HEAD_DIM), f32)
        for at in range(0, length, BLOCK):
            rows = slice(at, at + BLOCK)
            grad = grad_ref[rows, columns]
            scores = against(key, query[rows])
            weights = jnp.exp(scores - lse_ref[head : head + 1, rows])
            prob_adj = against(value, grad)
            delta = jnp.sum(weights * prob_adj, axis=0, keepdims=True)
            score_adj = (weights * (prob_adj - delta)).astype(bf16)
            key_adj += times(score_adj, query[rows])
            value_adj += times(weights.astype(bf16), grad)
            out_ref[rows, columns] = (times(key_t, score_adj) * scaling).T.astype(bf16)
        out_ref[:, part + columns.start : part + columns.stop] = key_adj.astype(bf16)
        out_ref[:, 2 * part + columns.start : 2 * part + columns.stop] = value_adj.astype(bf16)


def attend_forward(mixed, scaling):
    length, part = mixed.shape[0], mixed.shape[1] // 3
    pairs = part * length * length
    return pl.pallas_call(
        functools.partial(forward_kernel, scaling),
        out_shape=(
            jax.ShapeDtypeStruct((length, part), bf16),
            jax.ShapeDtypeStruct((8, length), f32),
        ),
        compiler_params=pltpu.CompilerParams(vmem_limit_bytes=40 * 2**20),
        cost_estimate=pl.CostEstimate(
            flops=16 * pairs, bytes_accessed=8 * part * length, transcendentals=pairs // HEAD_DIM
        ),
    )(mixed)


def attend_backward(mixed, lse, grad, scaling):
    length, part = grad.shape
    pairs = part * length * length
    return pl.pallas_call(
        functools.partial(backward_kernel, scaling),
        out_shape=jax.ShapeDtypeStruct(mixed.shape, bf16),
        compiler_params=pltpu.CompilerParams(vmem_limit_bytes=40 * 2**20),
        cost_estimate=pl.CostEstimate(
            flops=40 * pairs, bytes_accessed=16 * part * length, transcendentals=pairs // HEAD_DIM
        ),
    )(mixed, lse, grad)


def shards(
    tokens,
    input_weight,
    query_value_bias,
    output_weight,
    output_bias,
    expand_weight,
    expand_bias,
    reduce_weight,
    reduce_bias,
    first_gain,
    first_shift,
    second_gain,
    second_shift,
    attention_scale,
    feedforward_scale,
    cotangent,
):
    _, rows, width = tokens.shape
    units = reduce_weight.shape[0]
    part = output_weight.shape[0]
    group = 8
    length = group * rows
    half = part // 2
    scaling = HEAD_DIM ** (-0.5)
    me = lax.axis_index("z") * 2 + lax.axis_index("yl")
    x, core = lax.axis_index("x"), lax.axis_index("core")

    own = tokens[0]
    extra = 8
    offset, small = 0, 0
    for vector in (
        query_value_bias,
        output_bias,
        reduce_bias,
        first_gain,
        first_shift,
        second_gain,
        second_shift,
        attention_scale,
        feedforward_scale,
        expand_bias,
    ):
        small = small + place(vector, offset, (extra, width))
        offset += vector.shape[0]
    band = part // 8
    w = input_weight.reshape(8, band, 3, group, part).transpose(3, 2, 1, 0, 4).reshape(group, 3 * band, width)
    here = jnp.concatenate([own, small], axis=0)
    blocks = jnp.concatenate([jnp.broadcast_to(here[None], (group, *here.shape)), w], axis=1)

    up_half = lax.dynamic_slice_in_dim(expand_weight, core * half, half, 0)
    up_half = pick(up_half.reshape(half, group, NX, part), x, 2).reshape(half, width)
    down_half = lax.dynamic_slice_in_dim(reduce_weight, x * part + core * half, half, 0)
    out_half = lax.dynamic_slice_in_dim(output_weight, core * half, half, 0)
    w = jnp.concatenate([up_half, down_half, out_half], axis=0)
    blocks, other = lax.optimization_barrier((blocks, swap(w, "yl")))
    columns = gather_column(w, other)
    upstreams = gather_x(cotangent[0]).astype(f32)

    blocks = trade(blocks, SHARD)
    all_tokens = blocks[:, :rows].reshape(length, width).astype(f32)
    smalls = blocks[:, rows : rows + 2].reshape(group, 2 * width).astype(f32)
    in_w = blocks[:, rows + extra :].reshape(group, 3, band, 8, part).transpose(0, 3, 2, 1, 4)
    in_w = in_w.reshape(width, 3 * part)
    pair_bias = smalls[:, : 2 * part].reshape(2 * width)
    out_bias, down_bias, gain_one, shift_one, gain_two, shift_two, scale_one, scale_two = [
        smalls[:, (2 + j) * part : (3 + j) * part].reshape(width) for j in range(8)
    ]
    at = 10 * part
    up_bias = pick(smalls[:, at : at + units].reshape(group, NX, part), x, 1).reshape(width)
    bias = jnp.concatenate(
        [
            lax.dynamic_slice(pair_bias, (me * part,), (part,)),
            jnp.zeros((part,), f32),
            lax.dynamic_slice(pair_bias, (width + me * part,), (part,)),
        ]
    )

    local = own.astype(f32)
    normal_one = normalised(all_tokens)
    hidden = (normal_one * gain_one + shift_one).astype(bf16)
    mixed = (times(hidden, in_w) + bias).astype(bf16)
    attended, lse = attend_forward(mixed, scaling)
    columns = [after_that(c, attended) for c in columns]
    columns = columns + [swap(c, "core") for c in columns]
    up_w, down_w, out_w = assemble(columns, lax.axis_index("z"), core, width)
    attended = trade(attended.reshape(group, rows, part), SHARD)
    attended = attended.transpose(1, 0, 2).reshape(rows, width)
    branch = times(attended, out_w) + out_bias
    after = local + scale_one * branch

    second_own = layer_norm(after, gain_two, shift_two).astype(bf16)
    second = gather_x(second_own)
    down_adj = (scale_two * upstreams).astype(bf16)

    pre = times(second, up_w) + up_bias
    act, gelu_pull = jax.vjp(exact_gelu, pre)
    act = act.astype(bf16)
    pre_adj = gelu_pull(against(down_adj, down_w))[0].astype(bf16)
    second_adj = return_x(against(pre_adj, up_w).astype(bf16).reshape(NX, rows, width))

    def add(mine, other, axis):
        return (mine.astype(f32) + swap(other.astype(bf16), axis).astype(f32)).astype(bf16)

    def core_sum(array):
        return add(pick(array, core, 1), pick(array, 1 - core, 1), "core")

    pair = jnp.stack(
        [
            core_sum(g.astype(bf16).reshape(group, 2, half, width))
            for g in (across(act, down_adj), across(second, pre_adj))
        ],
        axis=1,
    )
    second_adj = after_that(second_adj, pair)
    down_part = times(act, down_w)
    arrived = send_z(pair.reshape(NZ, 2, part, width))

    upstream = cotangent[0].astype(f32)
    _, norm_pull = jax.vjp(layer_norm, after, gain_two, shift_two)
    after_inner, gain_two_adj, shift_two_adj = norm_pull(second_adj)
    after_adj = upstream + after_inner
    branch_adj = (scale_one * after_adj).astype(bf16)

    attended_adj = against(branch_adj, out_w).astype(bf16)
    attended_adj = trade(attended_adj.reshape(rows, group, part).transpose(1, 0, 2), SHARD)
    mixed_adj = attend_backward(mixed, lse, attended_adj.reshape(length, part), scaling)
    in_weight_adj = across(hidden, mixed_adj)
    hidden_part = against(mixed_adj, in_w)
    hidden_sent = trade(hidden_part.astype(bf16).reshape(group, rows, width), SHARD)

    piece = part // 8

    def chip_rows(array):
        return core_sum(array.reshape(group, 2, NX, piece, array.shape[-1]))

    def x_sum(array):
        return return_x([pick(array, (x + k) % NX, 1) for k in range(NX)]).astype(bf16)

    out_sum = x_sum(chip_rows(across(attended, branch_adj).astype(bf16)))

    sums = jnp.sum(mixed_adj.astype(f32), axis=0)
    pairs = jnp.zeros((width,), f32)
    pairs = lax.dynamic_update_slice(pairs, sums[:part], ((me // 2) * part,))
    pairs = lax.dynamic_update_slice(pairs, sums[2 * part :], (width // 2 + (me // 2) * part,))
    even = (me % 2 == 0).astype(f32)
    up_sums = jnp.sum(pre_adj.astype(f32), axis=0)
    vectors = [
        jnp.sum(branch_adj.astype(f32), axis=0),
        jnp.sum((scale_two * upstream).astype(bf16).astype(f32), axis=0),
        jnp.sum(hidden_part * normal_one, axis=0),
        jnp.sum(hidden_part, axis=0),
        gain_two_adj,
        shift_two_adj,
        jnp.sum(after_adj * branch, axis=0),
        jnp.sum(upstreams * down_part, axis=0) + jnp.sum(upstream, axis=0) * down_bias,
        pairs * even,
        pairs * (1 - even),
        *[up_sums * (x == j).astype(f32) for j in range(NX)],
    ]
    columns = jnp.stack(vectors).astype(bf16).T
    columns = jnp.pad(columns, ((0, 0), (0, part - columns.shape[1])))
    yl = lax.axis_index("yl")
    last = chip_rows(jnp.concatenate([in_weight_adj.astype(bf16), columns], axis=1))
    pair = total(jnp.stack(after_that(arrived, last))).astype(bf16)
    down = down_part.astype(bf16).reshape(NX, rows, width)
    down = return_x(after_that(down, last)) + down_bias
    layer_output = (after + scale_two * down).astype(bf16)
    pair = add(pick(pair, yl), pick(pair, 1 - yl), "yl")
    last = jnp.concatenate([x_sum(last), out_sum], axis=2)
    hidden_adj = total(after_that(hidden_sent, last))
    _, first_pull = jax.vjp(lambda v: normalised(v) * gain_one, local)
    tokens_adjoint = (after_adj + first_pull(hidden_adj)[0]).astype(bf16)
    pair = add(pair, pair, "yh")
    last = trade(after_that(add(last, last, "yh"), hidden_sent), SHARD)
    matrix = last[:, :, : 3 * part].reshape(group, piece, 3, part).transpose(1, 2, 0, 3).reshape(piece, 3 * width)
    sums = total(last[:, :, 3 * part :]).astype(bf16)
    last = arrivals(jnp.concatenate([matrix, sums], axis=1))
    reduce_weight_adj, expand_weight_adj = finish_pair(arrivals(pair), x, core, part, width)
    input_weight_adj, output_weight_adj, vectors = finish(last, x, core, part, width)

    return (
        layer_output[None],
        tokens_adjoint[None],
        input_weight_adj,
        vectors[8:10].reshape(2 * part),
        output_weight_adj,
        vectors[0],
        expand_weight_adj,
        vectors[10:14].reshape(units),
        reduce_weight_adj,
        vectors[1],
        *[vectors[j] for j in range(2, 8)],
    )


def solution(mesh):
    fine = Mesh(mesh.devices.reshape(2, NX, 2, NZ, 2), REP + SHARD)
    rows = P(REP, SHARD, None)
    matrix, vector = P(SHARD, None), P(SHARD)
    placed = (
        rows,
        matrix,
        vector,
        matrix,
        vector,
        matrix,
        vector,
        matrix,
        *[vector] * 7,
        rows,
    )
    return jax.shard_map(
        shards,
        mesh=fine,
        in_specs=placed,
        out_specs=(
            rows,
            rows,
            matrix,
            vector,
            matrix,
            vector,
            matrix,
            vector,
            matrix,
            *[vector] * 7,
        ),
        check_vma=False,
    )
```

```python
import functools

import jax
import jax.numpy as jnp
from jax import lax
from jax.experimental import pallas as pl
from jax.experimental.pallas import tpu as pltpu
from jax.sharding import Mesh, PartitionSpec as P

HEAD_DIM = 64
EPSILON = 1e-06
SHARD = ("z", "yl")
REP = ("yh", "x", "core")
NZ, NX = 4, 4
f32 = jnp.float32
bf16 = jnp.bfloat16


def normalised(values):
    mean = jnp.mean(values, axis=-1, keepdims=True)
    centred = values - mean
    variance = jnp.mean(centred * centred, axis=-1, keepdims=True)
    return centred * lax.rsqrt(variance + EPSILON)


def layer_norm(values, gain, shift):
    return normalised(values) * gain + shift


def exact_gelu(values):
    return jax.nn.gelu(values, approximate=False)


def times(left, right):
    return jnp.dot(left, right, preferred_element_type=f32)


def against(left, right):
    return lax.dot_general(left, right, (((1,), (1,)), ((), ())), preferred_element_type=f32)


def across(left, right):
    return lax.dot_general(left, right, (((0,), (0,)), ((), ())), preferred_element_type=f32)


SWAP = [(0, 1), (1, 0)]


def swap(block, axis):
    return lax.ppermute(block, axis, SWAP)


def trade(parts, axes):
    return lax.all_to_all(parts, axes, split_axis=0, concat_axis=0, tiled=True)


def gather(block, axes, n):
    return trade(jnp.broadcast_to(block[None], (n, *block.shape)), axes)


def pick(array, index, axis=0):
    return lax.dynamic_index_in_dim(array, index, axis, keepdims=False)


def both_cores(half, axis):
    other = swap(half, "core")
    first = lax.axis_index("core") == 0
    return jnp.concatenate([jnp.where(first, half, other), jnp.where(first, other, half)], axis=axis)


def ahead(block, axis, n, k):
    return lax.ppermute(block, axis, [((i + k) % n, i) for i in range(n)])


def give(block, axis, n, k):
    return lax.ppermute(block, axis, [(i, (i + k) % n) for i in range(n)])


def gather_x(block):
    return jnp.concatenate([block] + [ahead(block, "x", NX, k) for k in range(1, NX)], axis=0)


def return_x(parts):
    sent = [give(parts[k], "x", NX, k) for k in range(1, NX)]
    return parts[0].astype(f32) + sum(p.astype(f32) for p in sent)


def gather_column(block, other):
    low = lax.axis_index("yl") == 0
    column = jnp.stack([jnp.where(low, block, other), jnp.where(low, other, block)])
    return [column] + [ahead(column, "z", NZ, k) for k in range(1, NZ)]


def send_z(parts):
    z = lax.axis_index("z")
    return [pick(parts, z)] + [give(pick(parts, (z + k) % NZ), "z", NZ, k) for k in range(1, NZ)]


def arrivals(block, earlier=None):
    blocks = [block] + [ahead(block, "x", NX, k) for k in range(1, NX)]
    if earlier is not None:
        blocks = after_that(blocks, earlier)
    return blocks + [swap(b, "core") for b in blocks]


def place(vector, offset, shape):
    row, column = divmod(offset, shape[1])
    size = vector.shape[0]
    return jnp.pad(vector.reshape(1, size), ((row, shape[0] - row - 1), (column, shape[1] - column - size)))


def after_that(value, earlier):
    return lax.optimization_barrier((value, earlier))[0]


def total(parts):
    return jnp.sum(parts.astype(f32), axis=0)


VMEM = pl.BlockSpec(memory_space=pltpu.VMEM)


def assemble_kernel(place_ref, *refs):
    columns, outs = refs[:-3], refs[-3:]
    z, core = place_ref[0], place_ref[1]
    half = columns[0].shape[1] // 3
    for j, column in enumerate(columns):
        block, side = j % NZ, core if j < NZ else 1 - core
        for y in range(2):
            first = ((lax.rem(z + block, NZ) * 2 + y) * 2 + side) * half
            rows = pl.ds(pl.multiple_of(first, half), half)
            for out, at in zip(outs, range(0, 3 * half, half)):
                out[rows, :] = column[y, at : at + half, :]


def assemble(columns, z, core, width):
    whole = jax.ShapeDtypeStruct((width, width), bf16)
    return pl.pallas_call(
        assemble_kernel,
        out_shape=(whole, whole, whole),
        in_specs=[pl.BlockSpec(memory_space=pltpu.SMEM)] + [VMEM] * len(columns),
        out_specs=(VMEM, VMEM, VMEM),
        compiler_params=pltpu.CompilerParams(vmem_limit_bytes=32 * 2**20),
        cost_estimate=pl.CostEstimate(flops=0, bytes_accessed=12 * width * width, transcendentals=0),
    )(jnp.stack([z, core]).astype(jnp.int32), *columns)


def finish_kernel(place_ref, *refs):
    pieces, (in_ref, out_ref, vector_ref, scratch) = refs[:-4], refs[-4:]
    x, core = place_ref[0], place_ref[1]
    piece, width, part = pieces[0].shape[0], out_ref.shape[1], scratch.shape[1]
    for j, ref in enumerate(pieces):
        side = core if j < NX else 1 - core
        first = (side * NX + lax.rem(x + j % NX, NX)) * piece
        rows = pl.ds(pl.multiple_of(first, piece), piece)
        in_ref[rows, :] = ref[:, : 3 * width].astype(f32)
        scratch[rows, :] = ref[:, 3 * width : 3 * width + part].astype(f32)
        out_ref[rows, :] = ref[:, 3 * width + part :].astype(f32)
    vector_ref[...] = scratch[...].T


def finish(pieces, x, core, part, width):
    return pl.pallas_call(
        finish_kernel,
        out_shape=(
            jax.ShapeDtypeStruct((part, 3 * width), f32),
            jax.ShapeDtypeStruct((part, width), f32),
            jax.ShapeDtypeStruct((part, part), f32),
        ),
        in_specs=[pl.BlockSpec(memory_space=pltpu.SMEM)] + [VMEM] * len(pieces),
        out_specs=(VMEM, VMEM, VMEM),
        scratch_shapes=[pltpu.VMEM((part, part), f32)],
        compiler_params=pltpu.CompilerParams(vmem_limit_bytes=16 * 2**20),
        cost_estimate=pl.CostEstimate(flops=0, bytes_accessed=24 * part * width, transcendentals=0),
    )(jnp.stack([x, core]).astype(jnp.int32), *pieces)


def finish_pair_kernel(place_ref, *refs):
    pieces, (down_ref, up_ref) = refs[:-2], refs[-2:]
    x, core = place_ref[0], place_ref[1]
    part, width = pieces[0].shape
    half = part // 2
    for j, ref in enumerate(pieces):
        side = core if j < NX else 1 - core
        chip = lax.rem(x + j % NX, NX)
        first = (chip * 2 + side) * half
        down_ref[pl.ds(pl.multiple_of(first, half), half), :] = ref[:half, :].astype(f32)
        rows = pl.ds(pl.multiple_of(side * half, half), half)
        for s in range(width // part):
            at = pl.multiple_of((s * NX + chip) * part, part)
            up_ref[rows, pl.ds(at, part)] = ref[half:, s * part : (s + 1) * part].astype(f32)


def finish_pair(pieces, x, core, part, width):
    return pl.pallas_call(
        finish_pair_kernel,
        out_shape=(
            jax.ShapeDtypeStruct((NX * part, width), f32),
            jax.ShapeDtypeStruct((part, NX * width), f32),
        ),
        in_specs=[pl.BlockSpec(memory_space=pltpu.SMEM)] + [VMEM] * len(pieces),
        out_specs=(VMEM, VMEM),
        compiler_params=pltpu.CompilerParams(vmem_limit_bytes=16 * 2**20),
        cost_estimate=pl.CostEstimate(flops=0, bytes_accessed=48 * part * width, transcendentals=0),
    )(jnp.stack([x, core]).astype(jnp.int32), *pieces)


BLOCK = 256


def head_parts(mixed_ref, head, part):
    return [
        mixed_ref[:, j * part + head * HEAD_DIM : j * part + (head + 1) * HEAD_DIM] for j in range(3)
    ]


def forward_kernel(scaling, mixed_ref, attended_ref, lse_ref):
    length, part = attended_ref.shape
    for head in range(part // HEAD_DIM):
        query, key, value = head_parts(mixed_ref, head, part)
        query = query * jnp.asarray(scaling, bf16)
        value_t = value.T
        for at in range(0, length, BLOCK):
            scores = against(key, query[at : at + BLOCK])
            most = jnp.max(scores, axis=0, keepdims=True)
            weights = jnp.exp(scores - most)
            count = jnp.sum(weights, axis=0, keepdims=True)
            probs = (weights * (1.0 / count)).astype(bf16)
            attended_ref[at : at + BLOCK, head * HEAD_DIM : (head + 1) * HEAD_DIM] = (
                times(value_t, probs).T.astype(bf16)
            )
            lse_ref[head : head + 1, at : at + BLOCK] = most + jnp.log(count)


def backward_kernel(scaling, mixed_ref, lse_ref, grad_ref, out_ref):
    length, part = grad_ref.shape
    for head in range(part // HEAD_DIM):
        query, key, value = head_parts(mixed_ref, head, part)
        query = query * jnp.asarray(scaling, bf16)
        key_t = key.T
        columns = slice(head * HEAD_DIM, (head + 1) * HEAD_DIM)
        key_adj = jnp.zeros((length, HEAD_DIM), f32)
        value_adj = jnp.zeros((length, HEAD_DIM), f32)
        for at in range(0, length, BLOCK):
            rows = slice(at, at + BLOCK)
            grad = grad_ref[rows, columns]
            scores = against(key, query[rows])
            weights = jnp.exp(scores - lse_ref[head : head + 1, rows])
            prob_adj = against(value, grad)
            delta = jnp.sum(weights * prob_adj, axis=0, keepdims=True)
            score_adj = (weights * (prob_adj - delta)).astype(bf16)
            key_adj += times(score_adj, query[rows])
            value_adj += times(weights.astype(bf16), grad)
            out_ref[rows, columns] = (times(key_t, score_adj) * scaling).T.astype(bf16)
        out_ref[:, part + columns.start : part + columns.stop] = key_adj.astype(bf16)
        out_ref[:, 2 * part + columns.start : 2 * part + columns.stop] = value_adj.astype(bf16)


def attend_forward(mixed, scaling):
    length, part = mixed.shape[0], mixed.shape[1] // 3
    pairs = part * length * length
    return pl.pallas_call(
        functools.partial(forward_kernel, scaling),
        out_shape=(
            jax.ShapeDtypeStruct((length, part), bf16),
            jax.ShapeDtypeStruct((8, length), f32),
        ),
        compiler_params=pltpu.CompilerParams(vmem_limit_bytes=40 * 2**20),
        cost_estimate=pl.CostEstimate(
            flops=16 * pairs, bytes_accessed=8 * part * length, transcendentals=pairs // HEAD_DIM
        ),
    )(mixed)


def attend_backward(mixed, lse, grad, scaling):
    length, part = grad.shape
    pairs = part * length * length
    return pl.pallas_call(
        functools.partial(backward_kernel, scaling),
        out_shape=jax.ShapeDtypeStruct(mixed.shape, bf16),
        compiler_params=pltpu.CompilerParams(vmem_limit_bytes=40 * 2**20),
        cost_estimate=pl.CostEstimate(
            flops=40 * pairs, bytes_accessed=16 * part * length, transcendentals=pairs // HEAD_DIM
        ),
    )(mixed, lse, grad)


def shards(
    tokens,
    input_weight,
    query_value_bias,
    output_weight,
    output_bias,
    expand_weight,
    expand_bias,
    reduce_weight,
    reduce_bias,
    first_gain,
    first_shift,
    second_gain,
    second_shift,
    attention_scale,
    feedforward_scale,
    cotangent,
):
    _, rows, width = tokens.shape
    units = reduce_weight.shape[0]
    part = output_weight.shape[0]
    group = 8
    length = group * rows
    half = part // 2
    scaling = HEAD_DIM ** (-0.5)
    me = lax.axis_index("z") * 2 + lax.axis_index("yl")
    x, core = lax.axis_index("x"), lax.axis_index("core")

    own = tokens[0]
    extra = 8
    offset, small = 0, 0
    for vector in (
        query_value_bias,
        output_bias,
        reduce_bias,
        first_gain,
        first_shift,
        second_gain,
        second_shift,
        attention_scale,
        feedforward_scale,
        expand_bias,
    ):
        small = small + place(vector, offset, (extra, width))
        offset += vector.shape[0]
    band = part // 8
    w = input_weight.reshape(8, band, 3, group, part).transpose(3, 2, 1, 0, 4).reshape(group, 3 * band, width)
    here = jnp.concatenate([own, small], axis=0)
    blocks = jnp.concatenate([jnp.broadcast_to(here[None], (group, *here.shape)), w], axis=1)

    up_half = lax.dynamic_slice_in_dim(expand_weight, core * half, half, 0)
    up_half = pick(up_half.reshape(half, group, NX, part), x, 2).reshape(half, width)
    down_half = lax.dynamic_slice_in_dim(reduce_weight, x * part + core * half, half, 0)
    out_half = lax.dynamic_slice_in_dim(output_weight, core * half, half, 0)
    w = jnp.concatenate([up_half, down_half, out_half], axis=0)
    blocks, other = lax.optimization_barrier((blocks, swap(w, "yl")))
    columns = gather_column(w, other)
    upstreams = gather_x(cotangent[0]).astype(f32)

    blocks = trade(blocks, SHARD)
    all_tokens = blocks[:, :rows].reshape(length, width).astype(f32)
    smalls = blocks[:, rows : rows + 2].reshape(group, 2 * width).astype(f32)
    in_w = blocks[:, rows + extra :].reshape(group, 3, band, 8, part).transpose(0, 3, 2, 1, 4)
    in_w = in_w.reshape(width, 3 * part)
    pair_bias = smalls[:, : 2 * part].reshape(2 * width)
    out_bias, down_bias, gain_one, shift_one, gain_two, shift_two, scale_one, scale_two = [
        smalls[:, (2 + j) * part : (3 + j) * part].reshape(width) for j in range(8)
    ]
    at = 10 * part
    up_bias = pick(smalls[:, at : at + units].reshape(group, NX, part), x, 1).reshape(width)
    bias = jnp.concatenate(
        [
            lax.dynamic_slice(pair_bias, (me * part,), (part,)),
            jnp.zeros((part,), f32),
            lax.dynamic_slice(pair_bias, (width + me * part,), (part,)),
        ]
    )

    local = own.astype(f32)
    normal_one = normalised(all_tokens)
    hidden = (normal_one * gain_one + shift_one).astype(bf16)
    mixed = (times(hidden, in_w) + bias).astype(bf16)
    attended, lse = attend_forward(mixed, scaling)
    columns = [after_that(c, attended) for c in columns]
    columns = columns + [swap(c, "core") for c in columns]
    up_w, down_w, out_w = assemble(columns, lax.axis_index("z"), core, width)
    attended = trade(attended.reshape(group, rows, part), SHARD)
    attended = attended.transpose(1, 0, 2).reshape(rows, width)
    branch = times(attended, out_w) + out_bias
    after = local + scale_one * branch

    second_own = layer_norm(after, gain_two, shift_two).astype(bf16)
    second = gather_x(second_own)
    down_adj = (scale_two * upstreams).astype(bf16)

    pre = times(second, up_w) + up_bias
    act, gelu_pull = jax.vjp(exact_gelu, pre)
    act = act.astype(bf16)
    pre_adj = gelu_pull(against(down_adj, down_w))[0].astype(bf16)
    second_adj = return_x(against(pre_adj, up_w).astype(bf16).reshape(NX, rows, width))

    def add(mine, other, axis):
        return (mine.astype(f32) + swap(other.astype(bf16), axis).astype(f32)).astype(bf16)

    def core_sum(array):
        return add(pick(array, core, 1), pick(array, 1 - core, 1), "core")

    pair = jnp.stack(
        [
            core_sum(g.astype(bf16).reshape(group, 2, half, width))
            for g in (across(act, down_adj), across(second, pre_adj))
        ],
        axis=1,
    )
    second_adj = after_that(second_adj, pair)
    down_part = times(act, down_w)
    arrived = send_z(pair.reshape(NZ, 2, part, width))

    upstream = cotangent[0].astype(f32)
    _, norm_pull = jax.vjp(layer_norm, after, gain_two, shift_two)
    after_inner, gain_two_adj, shift_two_adj = norm_pull(second_adj)
    after_adj = upstream + after_inner
    branch_adj = (scale_one * after_adj).astype(bf16)

    attended_adj = against(branch_adj, out_w).astype(bf16)
    attended_adj = trade(attended_adj.reshape(rows, group, part).transpose(1, 0, 2), SHARD)
    piece = part // 8

    def chip_rows(array):
        return core_sum(array.reshape(group, 2, NX, piece, array.shape[-1]))

    def x_sum(array):
        return return_x([pick(array, (x + k) % NX, 1) for k in range(NX)]).astype(bf16)

    out_sum = x_sum(chip_rows(across(attended, branch_adj).astype(bf16)))

    yl = lax.axis_index("yl")
    pair = total(jnp.stack(arrived)).astype(bf16)
    attended_adj, pair = lax.optimization_barrier((attended_adj, pair))
    mixed_adj = attend_backward(mixed, lse, attended_adj.reshape(length, part), scaling)
    pair = add(pick(pair, yl), pick(pair, 1 - yl), "yl")
    mixed_adj, pair, out_sum = lax.optimization_barrier((mixed_adj, pair, out_sum))
    pair = add(pair, pair, "yh")
    in_weight_adj = across(hidden, mixed_adj)
    hidden_part = against(mixed_adj, in_w)
    hidden_sent = trade(hidden_part.astype(bf16).reshape(group, rows, width), SHARD)

    sums = jnp.sum(mixed_adj.astype(f32), axis=0)
    pairs = jnp.zeros((width,), f32)
    pairs = lax.dynamic_update_slice(pairs, sums[:part], ((me // 2) * part,))
    pairs = lax.dynamic_update_slice(pairs, sums[2 * part :], (width // 2 + (me // 2) * part,))
    even = (me % 2 == 0).astype(f32)
    up_sums = jnp.sum(pre_adj.astype(f32), axis=0)
    vectors = [
        jnp.sum(branch_adj.astype(f32), axis=0),
        jnp.sum((scale_two * upstream).astype(bf16).astype(f32), axis=0),
        jnp.sum(hidden_part * normal_one, axis=0),
        jnp.sum(hidden_part, axis=0),
        gain_two_adj,
        shift_two_adj,
        jnp.sum(after_adj * branch, axis=0),
        jnp.sum(upstreams * down_part, axis=0) + jnp.sum(upstream, axis=0) * down_bias,
        pairs * even,
        pairs * (1 - even),
        *[up_sums * (x == j).astype(f32) for j in range(NX)],
    ]
    columns = jnp.stack(vectors).astype(bf16).T
    columns = jnp.pad(columns, ((0, 0), (0, part - columns.shape[1])))
    last = chip_rows(after_that(jnp.concatenate([in_weight_adj.astype(bf16), columns], axis=1), pair))
    last = jnp.concatenate([x_sum(last), out_sum], axis=2)
    summed = last
    down = down_part.astype(bf16).reshape(NX, rows, width)
    down = return_x(after_that(down, summed)) + down_bias
    layer_output = (after + scale_two * down).astype(bf16)
    hidden_adj = total(after_that(hidden_sent, last))
    _, first_pull = jax.vjp(lambda v: normalised(v) * gain_one, local)
    tokens_adjoint = (after_adj + first_pull(hidden_adj)[0]).astype(bf16)
    last = trade(after_that(add(last, last, "yh"), hidden_sent), SHARD)
    matrix = last[:, :, : 3 * part].reshape(group, piece, 3, part).transpose(1, 2, 0, 3).reshape(piece, 3 * width)
    sums = total(last[:, :, 3 * part :]).astype(bf16)
    last = arrivals(jnp.concatenate([matrix, sums], axis=1))
    reduce_weight_adj, expand_weight_adj = finish_pair(arrivals(pair, summed), x, core, part, width)
    input_weight_adj, output_weight_adj, vectors = finish(last, x, core, part, width)

    return (
        layer_output[None],
        tokens_adjoint[None],
        input_weight_adj,
        vectors[8:10].reshape(2 * part),
        output_weight_adj,
        vectors[0],
        expand_weight_adj,
        vectors[10:14].reshape(units),
        reduce_weight_adj,
        vectors[1],
        *[vectors[j] for j in range(2, 8)],
    )


def solution(mesh):
    fine = Mesh(mesh.devices.reshape(2, NX, 2, NZ, 2), REP + SHARD)
    rows = P(REP, SHARD, None)
    matrix, vector = P(SHARD, None), P(SHARD)
    placed = (
        rows,
        matrix,
        vector,
        matrix,
        vector,
        matrix,
        vector,
        matrix,
        *[vector] * 7,
        rows,
    )
    return jax.shard_map(
        shards,
        mesh=fine,
        in_specs=placed,
        out_specs=(
            rows,
            rows,
            matrix,
            vector,
            matrix,
            vector,
            matrix,
            vector,
            matrix,
            *[vector] * 7,
        ),
        check_vma=False,
    )
```

```python
import functools

import jax
import jax.numpy as jnp
from jax import lax
from jax.experimental import pallas as pl
from jax.experimental.pallas import tpu as pltpu
from jax.sharding import Mesh, PartitionSpec as P

HEAD_DIM = 64
EPSILON = 1e-06
SHARD = ("z", "yl")
REP = ("yh", "x", "core")
NZ, NX = 4, 4
f32 = jnp.float32
bf16 = jnp.bfloat16


def normalised(values):
    mean = jnp.mean(values, axis=-1, keepdims=True)
    centred = values - mean
    variance = jnp.mean(centred * centred, axis=-1, keepdims=True)
    return centred * lax.rsqrt(variance + EPSILON)


def layer_norm(values, gain, shift):
    return normalised(values) * gain + shift


def exact_gelu(values):
    return jax.nn.gelu(values, approximate=False)


def times(left, right):
    return jnp.dot(left, right, preferred_element_type=f32)


def against(left, right):
    return lax.dot_general(left, right, (((1,), (1,)), ((), ())), preferred_element_type=f32)


def across(left, right):
    return lax.dot_general(left, right, (((0,), (0,)), ((), ())), preferred_element_type=f32)


SWAP = [(0, 1), (1, 0)]


def swap(block, axis):
    return lax.ppermute(block, axis, SWAP)


def trade(parts, axes):
    return lax.all_to_all(parts, axes, split_axis=0, concat_axis=0, tiled=True)


def gather(block, axes, n):
    return trade(jnp.broadcast_to(block[None], (n, *block.shape)), axes)


def pick(array, index, axis=0):
    return lax.dynamic_index_in_dim(array, index, axis, keepdims=False)


def both_cores(half, axis):
    other = swap(half, "core")
    first = lax.axis_index("core") == 0
    return jnp.concatenate([jnp.where(first, half, other), jnp.where(first, other, half)], axis=axis)


def ahead(block, axis, n, k):
    return lax.ppermute(block, axis, [((i + k) % n, i) for i in range(n)])


def give(block, axis, n, k):
    return lax.ppermute(block, axis, [(i, (i + k) % n) for i in range(n)])


def gather_x(block):
    return jnp.concatenate([block] + [ahead(block, "x", NX, k) for k in range(1, NX)], axis=0)


def return_x(parts):
    sent = [give(parts[k], "x", NX, k) for k in range(1, NX)]
    return parts[0].astype(f32) + sum(p.astype(f32) for p in sent)


def gather_column(block, other):
    low = lax.axis_index("yl") == 0
    column = jnp.stack([jnp.where(low, block, other), jnp.where(low, other, block)])
    return [column] + [ahead(column, "z", NZ, k) for k in range(1, NZ)]


def send_z(parts):
    z = lax.axis_index("z")
    return [pick(parts, z)] + [give(pick(parts, (z + k) % NZ), "z", NZ, k) for k in range(1, NZ)]


def arrivals(block, earlier=None):
    blocks = [block] + [ahead(block, "x", NX, k) for k in range(1, NX)]
    if earlier is not None:
        blocks = after_that(blocks, earlier)
    return blocks + [swap(b, "core") for b in blocks]


def place(vector, offset, shape):
    row, column = divmod(offset, shape[1])
    size = vector.shape[0]
    return jnp.pad(vector.reshape(1, size), ((row, shape[0] - row - 1), (column, shape[1] - column - size)))


def after_that(value, earlier):
    return lax.optimization_barrier((value, earlier))[0]


def total(parts):
    return jnp.sum(parts.astype(f32), axis=0)


VMEM = pl.BlockSpec(memory_space=pltpu.VMEM)


def assemble_kernel(place_ref, *refs):
    columns, outs = refs[:-3], refs[-3:]
    z, core = place_ref[0], place_ref[1]
    half = columns[0].shape[1] // 3
    for j, column in enumerate(columns):
        block, side = j % NZ, core if j < NZ else 1 - core
        for y in range(2):
            first = ((lax.rem(z + block, NZ) * 2 + y) * 2 + side) * half
            rows = pl.ds(pl.multiple_of(first, half), half)
            for out, at in zip(outs, range(0, 3 * half, half)):
                out[rows, :] = column[y, at : at + half, :]


def assemble(columns, z, core, width):
    whole = jax.ShapeDtypeStruct((width, width), bf16)
    return pl.pallas_call(
        assemble_kernel,
        out_shape=(whole, whole, whole),
        in_specs=[pl.BlockSpec(memory_space=pltpu.SMEM)] + [VMEM] * len(columns),
        out_specs=(VMEM, VMEM, VMEM),
        compiler_params=pltpu.CompilerParams(vmem_limit_bytes=32 * 2**20),
        cost_estimate=pl.CostEstimate(flops=0, bytes_accessed=12 * width * width, transcendentals=0),
    )(jnp.stack([z, core]).astype(jnp.int32), *columns)


def finish_kernel(place_ref, *refs):
    pieces, (in_ref, out_ref, vector_ref, scratch) = refs[:-4], refs[-4:]
    x, core = place_ref[0], place_ref[1]
    piece, width, part = pieces[0].shape[0], out_ref.shape[1], scratch.shape[1]
    for j, ref in enumerate(pieces):
        side = core if j < NX else 1 - core
        first = (side * NX + lax.rem(x + j % NX, NX)) * piece
        rows = pl.ds(pl.multiple_of(first, piece), piece)
        in_ref[rows, :] = ref[:, : 3 * width].astype(f32)
        scratch[rows, :] = ref[:, 3 * width : 3 * width + part].astype(f32)
        out_ref[rows, :] = ref[:, 3 * width + part :].astype(f32)
    vector_ref[...] = scratch[...].T


def finish(pieces, x, core, part, width):
    return pl.pallas_call(
        finish_kernel,
        out_shape=(
            jax.ShapeDtypeStruct((part, 3 * width), f32),
            jax.ShapeDtypeStruct((part, width), f32),
            jax.ShapeDtypeStruct((part, part), f32),
        ),
        in_specs=[pl.BlockSpec(memory_space=pltpu.SMEM)] + [VMEM] * len(pieces),
        out_specs=(VMEM, VMEM, VMEM),
        scratch_shapes=[pltpu.VMEM((part, part), f32)],
        compiler_params=pltpu.CompilerParams(vmem_limit_bytes=16 * 2**20),
        cost_estimate=pl.CostEstimate(flops=0, bytes_accessed=24 * part * width, transcendentals=0),
    )(jnp.stack([x, core]).astype(jnp.int32), *pieces)


def finish_pair_kernel(place_ref, *refs):
    pieces, (down_ref, up_ref) = refs[:-2], refs[-2:]
    x, core = place_ref[0], place_ref[1]
    part, width = pieces[0].shape
    half = part // 2
    for j, ref in enumerate(pieces):
        side = core if j < NX else 1 - core
        chip = lax.rem(x + j % NX, NX)
        first = (chip * 2 + side) * half
        down_ref[pl.ds(pl.multiple_of(first, half), half), :] = ref[:half, :].astype(f32)
        rows = pl.ds(pl.multiple_of(side * half, half), half)
        for s in range(width // part):
            at = pl.multiple_of((s * NX + chip) * part, part)
            up_ref[rows, pl.ds(at, part)] = ref[half:, s * part : (s + 1) * part].astype(f32)


def finish_pair(pieces, x, core, part, width):
    return pl.pallas_call(
        finish_pair_kernel,
        out_shape=(
            jax.ShapeDtypeStruct((NX * part, width), f32),
            jax.ShapeDtypeStruct((part, NX * width), f32),
        ),
        in_specs=[pl.BlockSpec(memory_space=pltpu.SMEM)] + [VMEM] * len(pieces),
        out_specs=(VMEM, VMEM),
        compiler_params=pltpu.CompilerParams(vmem_limit_bytes=16 * 2**20),
        cost_estimate=pl.CostEstimate(flops=0, bytes_accessed=48 * part * width, transcendentals=0),
    )(jnp.stack([x, core]).astype(jnp.int32), *pieces)


BLOCK = 256


def head_parts(mixed_ref, head, part):
    return [
        mixed_ref[:, j * part + head * HEAD_DIM : j * part + (head + 1) * HEAD_DIM] for j in range(3)
    ]


def forward_kernel(scaling, mixed_ref, attended_ref, lse_ref):
    length, part = attended_ref.shape
    for head in range(part // HEAD_DIM):
        query, key, value = head_parts(mixed_ref, head, part)
        query = query * jnp.asarray(scaling, bf16)
        value_t = value.T
        for at in range(0, length, BLOCK):
            scores = against(key, query[at : at + BLOCK])
            most = jnp.max(scores, axis=0, keepdims=True)
            weights = jnp.exp(scores - most)
            count = jnp.sum(weights, axis=0, keepdims=True)
            probs = (weights * (1.0 / count)).astype(bf16)
            attended_ref[at : at + BLOCK, head * HEAD_DIM : (head + 1) * HEAD_DIM] = (
                times(value_t, probs).T.astype(bf16)
            )
            lse_ref[head : head + 1, at : at + BLOCK] = most + jnp.log(count)


def backward_kernel(scaling, mixed_ref, lse_ref, grad_ref, out_ref):
    length, part = grad_ref.shape
    for head in range(part // HEAD_DIM):
        query, key, value = head_parts(mixed_ref, head, part)
        query = query * jnp.asarray(scaling, bf16)
        key_t = key.T
        columns = slice(head * HEAD_DIM, (head + 1) * HEAD_DIM)
        key_adj = jnp.zeros((length, HEAD_DIM), f32)
        value_adj = jnp.zeros((length, HEAD_DIM), f32)
        for at in range(0, length, BLOCK):
            rows = slice(at, at + BLOCK)
            grad = grad_ref[rows, columns]
            scores = against(key, query[rows])
            weights = jnp.exp(scores - lse_ref[head : head + 1, rows])
            prob_adj = against(value, grad)
            delta = jnp.sum(weights * prob_adj, axis=0, keepdims=True)
            score_adj = (weights * (prob_adj - delta)).astype(bf16)
            key_adj += times(score_adj, query[rows])
            value_adj += times(weights.astype(bf16), grad)
            out_ref[rows, columns] = (times(key_t, score_adj) * scaling).T.astype(bf16)
        out_ref[:, part + columns.start : part + columns.stop] = key_adj.astype(bf16)
        out_ref[:, 2 * part + columns.start : 2 * part + columns.stop] = value_adj.astype(bf16)


def attend_forward(mixed, scaling):
    length, part = mixed.shape[0], mixed.shape[1] // 3
    pairs = part * length * length
    return pl.pallas_call(
        functools.partial(forward_kernel, scaling),
        out_shape=(
            jax.ShapeDtypeStruct((length, part), bf16),
            jax.ShapeDtypeStruct((8, length), f32),
        ),
        compiler_params=pltpu.CompilerParams(vmem_limit_bytes=40 * 2**20),
        cost_estimate=pl.CostEstimate(
            flops=16 * pairs, bytes_accessed=8 * part * length, transcendentals=pairs // HEAD_DIM
        ),
    )(mixed)


def attend_backward(mixed, lse, grad, scaling):
    length, part = grad.shape
    pairs = part * length * length
    return pl.pallas_call(
        functools.partial(backward_kernel, scaling),
        out_shape=jax.ShapeDtypeStruct(mixed.shape, bf16),
        compiler_params=pltpu.CompilerParams(vmem_limit_bytes=40 * 2**20),
        cost_estimate=pl.CostEstimate(
            flops=40 * pairs, bytes_accessed=16 * part * length, transcendentals=pairs // HEAD_DIM
        ),
    )(mixed, lse, grad)


def shards(
    tokens,
    input_weight,
    query_value_bias,
    output_weight,
    output_bias,
    expand_weight,
    expand_bias,
    reduce_weight,
    reduce_bias,
    first_gain,
    first_shift,
    second_gain,
    second_shift,
    attention_scale,
    feedforward_scale,
    cotangent,
):
    _, rows, width = tokens.shape
    units = reduce_weight.shape[0]
    part = output_weight.shape[0]
    group = 8
    length = group * rows
    half = part // 2
    scaling = HEAD_DIM ** (-0.5)
    me = lax.axis_index("z") * 2 + lax.axis_index("yl")
    x, core = lax.axis_index("x"), lax.axis_index("core")

    own = tokens[0]
    extra = 8
    offset, small = 0, 0
    for vector in (
        query_value_bias,
        output_bias,
        reduce_bias,
        first_gain,
        first_shift,
        second_gain,
        second_shift,
        attention_scale,
        feedforward_scale,
        expand_bias,
    ):
        small = small + place(vector, offset, (extra, width))
        offset += vector.shape[0]
    band = part // 8
    w = input_weight.reshape(8, band, 3, group, part).transpose(3, 2, 1, 0, 4).reshape(group, 3 * band, width)
    here = jnp.concatenate([own, small], axis=0)
    blocks = jnp.concatenate([jnp.broadcast_to(here[None], (group, *here.shape)), w], axis=1)

    up_half = lax.dynamic_slice_in_dim(expand_weight, core * half, half, 0)
    up_half = pick(up_half.reshape(half, group, NX, part), x, 2).reshape(half, width)
    down_half = lax.dynamic_slice_in_dim(reduce_weight, x * part + core * half, half, 0)
    out_half = lax.dynamic_slice_in_dim(output_weight, core * half, half, 0)
    w = jnp.concatenate([up_half, down_half, out_half], axis=0)
    blocks, other = lax.optimization_barrier((blocks, swap(w, "yl")))
    columns = gather_column(w, other)
    upstreams = gather_x(cotangent[0]).astype(f32)

    blocks = trade(blocks, SHARD)
    all_tokens = blocks[:, :rows].reshape(length, width).astype(f32)
    smalls = blocks[:, rows : rows + 2].reshape(group, 2 * width).astype(f32)
    in_w = blocks[:, rows + extra :].reshape(group, 3, band, 8, part).transpose(0, 3, 2, 1, 4)
    in_w = in_w.reshape(width, 3 * part)
    pair_bias = smalls[:, : 2 * part].reshape(2 * width)
    out_bias, down_bias, gain_one, shift_one, gain_two, shift_two, scale_one, scale_two = [
        smalls[:, (2 + j) * part : (3 + j) * part].reshape(width) for j in range(8)
    ]
    at = 10 * part
    up_bias = pick(smalls[:, at : at + units].reshape(group, NX, part), x, 1).reshape(width)
    bias = jnp.concatenate(
        [
            lax.dynamic_slice(pair_bias, (me * part,), (part,)),
            jnp.zeros((part,), f32),
            lax.dynamic_slice(pair_bias, (width + me * part,), (part,)),
        ]
    )

    local = own.astype(f32)
    normal_one = normalised(all_tokens)
    hidden = (normal_one * gain_one + shift_one).astype(bf16)
    mixed = (times(hidden, in_w) + bias).astype(bf16)
    attended, lse = attend_forward(mixed, scaling)
    columns = [after_that(c, attended) for c in columns]
    columns = columns + [swap(c, "core") for c in columns]
    up_w, down_w, out_w = assemble(columns, lax.axis_index("z"), core, width)
    attended = trade(attended.reshape(group, rows, part), SHARD)
    attended = attended.transpose(1, 0, 2).reshape(rows, width)
    branch = times(attended, out_w) + out_bias
    after = local + scale_one * branch

    second_own = layer_norm(after, gain_two, shift_two).astype(bf16)
    second = gather_x(second_own)
    down_adj = (scale_two * upstreams).astype(bf16)

    pre = times(second, up_w) + up_bias
    act, gelu_pull = jax.vjp(exact_gelu, pre)
    act = act.astype(bf16)
    pre_adj = gelu_pull(against(down_adj, down_w))[0].astype(bf16)
    second_adj = return_x(against(pre_adj, up_w).astype(bf16).reshape(NX, rows, width))

    def add(mine, other, axis):
        return (mine.astype(f32) + swap(other.astype(bf16), axis).astype(f32)).astype(bf16)

    def core_sum(array):
        return add(pick(array, core, 1), pick(array, 1 - core, 1), "core")

    pair = jnp.stack(
        [
            core_sum(g.astype(bf16).reshape(group, 2, half, width))
            for g in (across(act, down_adj), across(second, pre_adj))
        ],
        axis=1,
    )
    second_adj = after_that(second_adj, pair)
    down_part = times(act, down_w)
    arrived = send_z(pair.reshape(NZ, 2, part, width))

    upstream = cotangent[0].astype(f32)
    _, norm_pull = jax.vjp(layer_norm, after, gain_two, shift_two)
    after_inner, gain_two_adj, shift_two_adj = norm_pull(second_adj)
    after_adj = upstream + after_inner
    branch_adj = (scale_one * after_adj).astype(bf16)

    attended_adj = against(branch_adj, out_w).astype(bf16)
    attended_adj = trade(attended_adj.reshape(rows, group, part).transpose(1, 0, 2), SHARD)
    piece = part // 8

    def chip_rows(array):
        return core_sum(array.reshape(group, 2, NX, piece, array.shape[-1]))

    def x_sum(array):
        return return_x([pick(array, (x + k) % NX, 1) for k in range(NX)]).astype(bf16)

    out_sum = x_sum(chip_rows(across(attended, branch_adj).astype(bf16)))

    yl = lax.axis_index("yl")
    pair = total(jnp.stack(arrived)).astype(bf16)
    attended_adj, pair = lax.optimization_barrier((attended_adj, pair))
    mixed_adj = attend_backward(mixed, lse, attended_adj.reshape(length, part), scaling)
    pair = add(pick(pair, yl), pick(pair, 1 - yl), "yl")
    mixed_adj, pair = lax.optimization_barrier((mixed_adj, pair))
    pair = add(pair, pair, "yh")
    in_weight_adj = across(hidden, mixed_adj)
    hidden_part = against(mixed_adj, in_w)
    hidden_sent = trade(hidden_part.astype(bf16).reshape(group, rows, width), SHARD)

    sums = jnp.sum(mixed_adj.astype(f32), axis=0)
    pairs = jnp.zeros((width,), f32)
    pairs = lax.dynamic_update_slice(pairs, sums[:part], ((me // 2) * part,))
    pairs = lax.dynamic_update_slice(pairs, sums[2 * part :], (width // 2 + (me // 2) * part,))
    even = (me % 2 == 0).astype(f32)
    up_sums = jnp.sum(pre_adj.astype(f32), axis=0)
    vectors = [
        jnp.sum(branch_adj.astype(f32), axis=0),
        jnp.sum((scale_two * upstream).astype(bf16).astype(f32), axis=0),
        jnp.sum(hidden_part * normal_one, axis=0),
        jnp.sum(hidden_part, axis=0),
        gain_two_adj,
        shift_two_adj,
        jnp.sum(after_adj * branch, axis=0),
        jnp.sum(upstreams * down_part, axis=0) + jnp.sum(upstream, axis=0) * down_bias,
        pairs * even,
        pairs * (1 - even),
        *[up_sums * (x == j).astype(f32) for j in range(NX)],
    ]
    columns = jnp.stack(vectors).astype(bf16).T
    columns = jnp.pad(columns, ((0, 0), (0, part - columns.shape[1])))
    last = chip_rows(after_that(jnp.concatenate([in_weight_adj.astype(bf16), columns], axis=1), pair))
    last = jnp.concatenate([x_sum(last), out_sum], axis=2)
    summed = last
    down = down_part.astype(bf16).reshape(NX, rows, width)
    down = return_x(after_that(down, summed)) + down_bias
    layer_output = (after + scale_two * down).astype(bf16)
    hidden_adj = total(after_that(hidden_sent, last))
    _, first_pull = jax.vjp(lambda v: normalised(v) * gain_one, local)
    tokens_adjoint = (after_adj + first_pull(hidden_adj)[0]).astype(bf16)
    last = trade(after_that(add(last, last, "yh"), hidden_sent), SHARD)
    matrix = last[:, :, : 3 * part].reshape(group, piece, 3, part).transpose(1, 2, 0, 3).reshape(piece, 3 * width)
    sums = total(last[:, :, 3 * part :]).astype(bf16)
    last = arrivals(jnp.concatenate([matrix, sums], axis=1))
    reduce_weight_adj, expand_weight_adj = finish_pair(arrivals(pair, summed), x, core, part, width)
    input_weight_adj, output_weight_adj, vectors = finish(last, x, core, part, width)

    return (
        layer_output[None],
        tokens_adjoint[None],
        input_weight_adj,
        vectors[8:10].reshape(2 * part),
        output_weight_adj,
        vectors[0],
        expand_weight_adj,
        vectors[10:14].reshape(units),
        reduce_weight_adj,
        vectors[1],
        *[vectors[j] for j in range(2, 8)],
    )


def solution(mesh):
    fine = Mesh(mesh.devices.reshape(2, NX, 2, NZ, 2), REP + SHARD)
    rows = P(REP, SHARD, None)
    matrix, vector = P(SHARD, None), P(SHARD)
    placed = (
        rows,
        matrix,
        vector,
        matrix,
        vector,
        matrix,
        vector,
        matrix,
        *[vector] * 7,
        rows,
    )
    return jax.shard_map(
        shards,
        mesh=fine,
        in_specs=placed,
        out_specs=(
            rows,
            rows,
            matrix,
            vector,
            matrix,
            vector,
            matrix,
            vector,
            matrix,
            *[vector] * 7,
        ),
        check_vma=False,
    )
```
